128 devices in a mesh: wide: 32 (over z, y, core), patch: 4 (over x).
Axes of the slice: x: 4, y: 4, z: 4, core: 2. Of those that a mesh axis runs over, the one named last changes fastest.
Arguments:
- grid_state: bfloat16 [84, 262144], P(None, ('wide', 'patch')), may hold values from -6 to 6
- cotangent: bfloat16 [84, 262144], P(None, ('wide', 'patch')), may hold values from -6 to 6
- encoder_weight: bfloat16 [84, 512], replicated, may hold values from -0.625 to 0.625
- norm_gain: bfloat16 [512], replicated, may hold values from 0.5 to 1.5
- query_weight: bfloat16 [512, 512], replicated
- key_weight: bfloat16 [512, 512], replicated
- value_weight: bfloat16 [512, 512], replicated, may hold values from -0.25 to 0.25
- output_weight: bfloat16 [512, 512], replicated, may hold values from -0.25 to 0.25
- decoder_weight: bfloat16 [512, 84], replicated, may hold values from -0.25 to 0.25
- grid_owner: int32 [262144], P(('wide', 'patch')), may hold values from 0 to 65535, as said below
- decode_node: int32 [262144], P(('wide', 'patch')), may hold values from 0 to 65535, as said below
- tile_pattern: int32 [512, 16], P(('wide', 'patch')), may hold values from 0 to 1, as said below
Outputs:
- denoised: bfloat16 [84, 262144], P(None, ('wide', 'patch'))
- state_grad: float32 [84, 262144], P(None, ('wide', 'patch'))
- encoder_grad: float32 [84, 512], replicated
The draws below stay inside these ranges and needn't reach their ends.
Inputs may be any that keep to these rules, and one draw needn't show every extreme that they name: `grid_owner`: the node of every grid point lies on a device with the same patch index. At most 128 grid points of one device belong to the nodes of one device, and on every device one such pair holds exactly 128. `decode_node`: the node of every grid point lies on a device with the same patch index. At most 128 grid points of one device read the nodes of one device, and on every device one such pair holds exactly 128. `tile_pattern`: every query tile attends to its own tile: entry (t, ((t * 128 // 512) % 4) * 4 + t % 4) is 1.
All inputs are finite; a program needn't handle non-finite values.
Results may differ from the reference program's by a relative error of at most 0.008.
Values may be sent and summed in bfloat16 or wider, within the bound.
No kernel may reach another device: no remote copies, remote signals or barrier semaphores. Data moves between devices by JAX's collectives and lax.ppermute only.
A program may use at most 192 MiB of HBM per device.

```python
import math
import jax
import jax.numpy as jnp
from jax import lax

V = 84
D = 512
HEADS = 4
HEAD = 128
TILE = 128
GRID_DEV = 2048
NODE_DEV = 512
PEERS = 32
GROUP = 4
CAP = 128
GRID = 262144
NODES = 65536


def route_table(key):

    def one_device(device):
        device_key = jax.random.fold_in(key, device)
        first_key, second_key, third_key, fourth_key = jax.random.split(device_key, 4)
        hot_peer = jax.random.randint(first_key, (), 0, PEERS)
        chosen = jax.random.permutation(second_key, (PEERS - 1) * CAP)[:GRID_DEV - CAP]
        others = chosen // CAP
        others = others + (others >= hot_peer).astype(jnp.int32)
        targets = jnp.concatenate([jnp.full((CAP,), hot_peer, jnp.int32), others.astype(jnp.int32)])
        shuffle = jax.random.permutation(third_key, GRID_DEV)
        targets = targets[shuffle]
        local = jax.random.randint(fourth_key, (GRID_DEV,), 0, NODE_DEV)
        return ((targets * GROUP + device % GROUP) * NODE_DEV + local).astype(jnp.int32)
    return jax.vmap(one_device)(jnp.arange(PEERS * GROUP, dtype=jnp.int32)).reshape(GRID_DEV * PEERS * GROUP)


def draw_grid_owner(key, part):
    key = jax.random.fold_in(key, 11)
    return route_table(key)


def draw_decode_node(key, part):
    key = jax.random.fold_in(key, 12)
    return route_table(key)


def draw_tile_pattern(key, part):
    key = jax.random.fold_in(key, 13)
    rows_count = NODES // TILE
    cols_count = GROUP * NODE_DEV // TILE
    random_bits = jax.random.randint(key, (rows_count, cols_count), 0, 2)
    tile_rows = lax.broadcasted_iota(jnp.int32, (rows_count, cols_count), 0)
    tile_cols = lax.broadcasted_iota(jnp.int32, (rows_count, cols_count), 1)
    own_col = tile_rows * TILE // NODE_DEV % GROUP * (NODE_DEV // TILE) + tile_rows % (NODE_DEV // TILE)
    return jnp.where(tile_cols == own_col, 1, random_bits).astype(jnp.int32)


def drawn_weight(key):
    base = jax.random.normal(key, (D, D), jnp.float32) * D ** (-0.5)
    return base.astype(jnp.bfloat16)


def draw_query_weight(key, part):
    key = jax.random.fold_in(key, 21)
    return drawn_weight(key)


def draw_key_weight(key, part):
    key = jax.random.fold_in(key, 22)
    return drawn_weight(key)


def block_levels(rng, dims, shards, smallest, top_value):
    def one(axis_at, parts):
        heights = jax.random.uniform(jax.random.fold_in(jax.random.fold_in(rng, 6), axis_at), (parts,), jnp.float32, smallest / len(shards), top_value / len(shards))
        return jnp.repeat(jnp.exp(heights), dims[axis_at] // parts).reshape((-1,) + (1,) * (len(dims) - axis_at - 1))

    gain = one(*shards[0])
    for cut in shards[1:]:
        gain = gain * one(*cut)
    return gain


def centred(key, extent, spread, most, shards=(), kind=jnp.bfloat16):
    array = spread * jax.random.normal(key, extent, jnp.float32)
    if shards:
        array = array * block_levels(key, extent, shards, -0.22, 0.18)
    return jnp.clip(array, -most, most).astype(kind)


def setup_inputs(seed: int = 0) -> dict:
    seeds = jax.random.split(jax.random.key(seed), 13)
    grid_state = centred(seeds[0], (V, GRID), 1.0, 6.0, ((1, 128),))
    cotangent = centred(seeds[1], (V, GRID), 1.0, 6.0, ((1, 128),))
    encoder_weight = centred(seeds[2], (V, D), V ** -0.5, 0.625)
    norm_gain = jnp.clip(1.0 + 0.1 * jax.random.normal(seeds[3], (D,), jnp.float32), 0.5, 1.5).astype(jnp.bfloat16)
    query_weight = draw_query_weight(jax.random.fold_in(seeds[12], 71), 0)
    key_weight = draw_key_weight(jax.random.fold_in(seeds[12], 71), 0)
    value_weight = centred(seeds[6], (D, D), D ** -0.5, 0.25)
    output_weight = centred(seeds[7], (D, D), D ** -0.5, 0.25)
    decoder_weight = centred(seeds[8], (D, V), D ** -0.5, 0.25)
    grid_owner = draw_grid_owner(jax.random.fold_in(seeds[12], 71), 0)
    decode_node = draw_decode_node(jax.random.fold_in(seeds[12], 71), 0)
    tile_pattern = draw_tile_pattern(jax.random.fold_in(seeds[12], 71), 0)
    return dict(grid_state=grid_state, cotangent=cotangent, encoder_weight=encoder_weight, norm_gain=norm_gain, query_weight=query_weight, key_weight=key_weight, value_weight=value_weight, output_weight=output_weight, decoder_weight=decoder_weight, grid_owner=grid_owner, decode_node=decode_node, tile_pattern=tile_pattern)


def attend(queries, keys, values, pattern, mixed_grad):
    query_rows = queries.shape[0]
    key_rows = keys.shape[0]
    scale = 1.0 / math.sqrt(HEAD)
    allowed = jnp.repeat(jnp.repeat(pattern > 0, TILE, axis=0), TILE, axis=1)
    query_heads = queries.astype(jnp.float32).reshape(query_rows, HEADS, HEAD)
    key_heads = keys.astype(jnp.float32).reshape(key_rows, HEADS, HEAD)
    value_heads = values.astype(jnp.float32).reshape(key_rows, HEADS, HEAD)
    grad_heads = mixed_grad.astype(jnp.float32).reshape(query_rows, HEADS, HEAD)
    scores = jnp.einsum('qhd,khd->hqk', query_heads, key_heads) * scale
    scores = jnp.where(allowed[None, :, :], scores, -1e+30)
    highest = lax.optimization_barrier(jnp.max(scores, axis=2, keepdims=True))
    weights = jnp.exp(scores - highest)
    probs = weights / lax.optimization_barrier(jnp.sum(weights, axis=2, keepdims=True))
    probs_bf = probs.astype(jnp.bfloat16)
    probs_back = probs_bf.astype(jnp.float32)
    mixed = jnp.einsum('hqk,khd->qhd', probs_back, value_heads).astype(jnp.bfloat16).reshape(query_rows, HEADS * HEAD)
    prob_grad = jnp.einsum('qhd,khd->hqk', grad_heads, value_heads)
    delta = lax.optimization_barrier(jnp.sum(probs * prob_grad, axis=2, keepdims=True))
    score_grad = (probs * (prob_grad - delta) * scale).astype(jnp.bfloat16).astype(jnp.float32)
    query_grad = jnp.einsum('hqk,khd->qhd', score_grad, key_heads).astype(jnp.bfloat16).reshape(query_rows, HEADS * HEAD)
    key_grad = jnp.einsum('hqk,qhd->khd', score_grad, query_heads).reshape(key_rows, HEADS * HEAD)
    value_grad = jnp.einsum('hqk,qhd->khd', probs_back, grad_heads).reshape(key_rows, HEADS * HEAD)
    return (mixed, query_grad, key_grad, value_grad)

def reference(grid_state, cotangent, encoder_weight, norm_gain, query_weight, key_weight, value_weight, output_weight, decoder_weight, grid_owner, decode_node, tile_pattern):
    highest_prec = lax.Precision.HIGHEST
    state_sum = jax.ops.segment_sum(grid_state.astype(jnp.float32).T, grid_owner, num_segments=NODES)
    cot_sum = jax.ops.segment_sum(cotangent.astype(jnp.float32).T, decode_node, num_segments=NODES)
    encoder_full = encoder_weight.astype(jnp.float32)
    start_rows = jnp.dot(state_sum, encoder_full, precision=highest_prec)
    inverse_rms = lax.rsqrt(lax.optimization_barrier(jnp.mean(start_rows * start_rows, axis=1, keepdims=True)) + 1e-05)
    gain_full = norm_gain.astype(jnp.float32)
    normed = (start_rows * inverse_rms * gain_full).astype(jnp.bfloat16)
    queries = jnp.dot(normed, query_weight, preferred_element_type=jnp.float32).astype(jnp.bfloat16)
    keys = jnp.dot(normed, key_weight, preferred_element_type=jnp.float32).astype(jnp.bfloat16)
    values = jnp.dot(normed, value_weight, preferred_element_type=jnp.float32).astype(jnp.bfloat16)
    top_grad = jnp.dot(cot_sum, decoder_weight.astype(jnp.float32).T, precision=highest_prec)
    top_grad_bf = top_grad.astype(jnp.bfloat16)
    mixed_grad = jnp.dot(top_grad_bf, output_weight.T, preferred_element_type=jnp.float32).astype(jnp.bfloat16)
    group_rows = GROUP * NODE_DEV
    group_tiles = group_rows // TILE

    def one_group(pieces):
        return attend(pieces[0], pieces[1], pieces[2], pieces[3], pieces[4])
    grouped = (queries.reshape(PEERS, group_rows, D), keys.reshape(PEERS, group_rows, D), values.reshape(PEERS, group_rows, D), tile_pattern.reshape(PEERS, group_tiles, group_tiles), mixed_grad.reshape(PEERS, group_rows, D))
    mixed, query_grad, key_grad, value_grad = lax.map(one_group, grouped)
    mixed = mixed.reshape(NODES, D)
    query_grad = query_grad.reshape(NODES, D)
    key_grad_bf = key_grad.reshape(NODES, D).astype(jnp.bfloat16)
    value_grad_bf = value_grad.reshape(NODES, D).astype(jnp.bfloat16)
    final_rows = start_rows + jnp.dot(mixed, output_weight, preferred_element_type=jnp.float32)
    final_bf = final_rows.astype(jnp.bfloat16)
    decoded_nodes = jnp.dot(final_bf, decoder_weight, preferred_element_type=jnp.float32)
    denoised = decoded_nodes[decode_node].T.astype(jnp.bfloat16)
    normed_grad = jnp.dot(query_grad, query_weight.T, preferred_element_type=jnp.float32)
    normed_grad = normed_grad + jnp.dot(key_grad_bf, key_weight.T, preferred_element_type=jnp.float32)
    normed_grad = normed_grad + jnp.dot(value_grad_bf, value_weight.T, preferred_element_type=jnp.float32)
    scaled_grad = normed_grad * gain_full
    start_grad = top_grad + inverse_rms * scaled_grad - start_rows * inverse_rms ** 3 * lax.optimization_barrier(jnp.mean(start_rows * scaled_grad, axis=1, keepdims=True))
    encoder_grad = jnp.dot(state_sum.T, start_grad, precision=highest_prec)
    state_grad = jnp.dot(start_grad, encoder_full.T, precision=highest_prec)[grid_owner].T
    return (denoised, state_grad, encoder_grad)
```

```python
import functools
import math

import jax
import jax.numpy as jnp
from jax import lax
from jax.experimental import pallas as pl
from jax.experimental.pallas import tpu as pltpu
from jax.sharding import PartitionSpec as P

HEADS = 4
HEAD = 128
TILE = 128
ROWS = 88
F32 = jnp.float32
BF16 = jnp.bfloat16
MIB = 1024 * 1024


def dot(a, b):
    return jnp.dot(a, b, preferred_element_type=F32)


def dot_nt(a, b):
    return lax.dot_general(a, b, (((1,), (1,)), ((), ())), preferred_element_type=F32)


def split(x):
    high = x.astype(BF16)
    return high, (x - high.astype(F32)).astype(BF16)


def call(kernel, outs, scratch, name, flops, *args, smem=()):
    specs = [
        pl.BlockSpec(memory_space=pltpu.SMEM if i in smem else pltpu.VMEM) for i in range(len(args))
    ]
    return pl.pallas_call(
        kernel,
        out_shape=[jax.ShapeDtypeStruct(s, d) for s, d in outs],
        in_specs=specs,
        out_specs=[pl.BlockSpec(memory_space=pltpu.VMEM) for _ in outs],
        scratch_shapes=scratch,
        compiler_params=pltpu.CompilerParams(vmem_limit_bytes=56 * MIB),
        cost_estimate=pl.CostEstimate(flops=flops, bytes_accessed=1 << 20, transcendentals=0),
        name=name,
    )(*args)


def slot_onehot(rank_ref, pair):
    grid_count = rank_ref.shape[1]
    level = lax.broadcasted_iota(jnp.int32, (TILE, grid_count), 0).astype(F32).astype(BF16)
    parts = []
    for k in range(2):
        row = rank_ref[pl.ds(2 * pair + k, 1), :].astype(BF16)
        parts.append(jnp.where(level == row, jnp.ones((), BF16), jnp.zeros((), BF16)))
    return jnp.concatenate(parts, axis=0)


def pack_kernel(
    shift, x_ref, c_ref, own_ref, dec_ref, out_ref, own_rank, dec_rank, wide_s, pay_o, pay_d
):
    variables, grid_count = x_ref.shape
    peers = out_ref.shape[0]
    node_mask = 511
    chunk = 256
    upper = jnp.where(
        lax.broadcasted_iota(jnp.int32, (chunk, chunk), 0)
        < lax.broadcasted_iota(jnp.int32, (chunk, chunk), 1),
        1.0,
        0.0,
    ).astype(BF16)
    for data, index, rank, pay in (
        (x_ref, own_ref, own_rank, pay_o),
        (c_ref, dec_ref, dec_rank, pay_d),
    ):
        carry = jnp.zeros((peers, 1), F32)
        for start in range(0, grid_count, chunk):
            span = pl.ds(start, chunk)
            nodes = index[:, span]
            hit = lax.broadcasted_iota(jnp.int32, (peers, chunk), 0) == (nodes >> shift)
            ones = jnp.where(hit, 1.0, 0.0)
            before = dot(ones.astype(BF16), upper) + carry
            rank[:, span] = jnp.where(hit, before, -1.0)
            carry = carry + jnp.sum(ones, axis=1, keepdims=True)
        local = index[...] & node_mask
        wide_s[0:variables, :] = data[...].astype(F32)
        wide_s[variables : variables + 1, :] = (local >> 1).astype(F32)
        wide_s[variables + 1 : variables + 2, :] = (local & 1).astype(F32)
        wide_s[variables + 2 : ROWS, :] = jnp.zeros((ROWS - variables - 2, grid_count), F32)
        pay[...] = wide_s[...].astype(BF16)

    def step(pair, _):
        for k, rank, pay in ((0, own_rank, pay_o), (1, dec_rank, pay_d)):
            got = dot_nt(pay[...], slot_onehot(rank, pair)).astype(BF16)
            out_ref[2 * pair, pl.ds(k * ROWS, ROWS), :] = got[:, :TILE]
            out_ref[2 * pair + 1, pl.ds(k * ROWS, ROWS), :] = got[:, TILE:]
        return 0

    lax.fori_loop(0, peers // 2, step, 0)


def sums_kernel(variables, recv_ref, state_ref, state_bf_ref, cot_ref, own_ref, dec_ref):
    peers = recv_ref.shape[0]
    node_count = state_ref.shape[1]
    nodes = lax.broadcasted_iota(jnp.int32, (node_count, TILE), 0)
    state_ref[...] = jnp.zeros_like(state_ref)
    cot_ref[...] = jnp.zeros_like(cot_ref)

    def step(pair, _):
        for k, total, index in ((0, state_ref, own_ref), (1, cot_ref, dec_ref)):
            data, picks = [], []
            for one in range(2):
                block = recv_ref[2 * pair + one, pl.ds(k * ROWS, ROWS), :]
                wide = block[80:ROWS].astype(F32)
                at = variables - 80
                slots = (2.0 * wide[at : at + 1] + wide[at + 1 : at + 2]).astype(jnp.int32)
                index[pl.ds(2 * pair + one, 1), :] = slots
                picks.append(jnp.where(nodes == slots, 1.0, 0.0).astype(BF16))
                data.append(block)
            total[...] += dot_nt(jnp.concatenate(data, axis=1), jnp.concatenate(picks, axis=1))
        return 0

    lax.fori_loop(0, peers // 2, step, 0)
    keep = lax.broadcasted_iota(jnp.int32, state_ref.shape, 0) < variables
    state_ref[...] = jnp.where(keep, state_ref[...], 0.0)
    cot_ref[...] = jnp.where(keep, cot_ref[...], 0.0)
    state_bf_ref[...] = state_ref[...].astype(BF16)


def norm_t(start, gain):
    inverse = lax.rsqrt(jnp.mean(start * start, axis=0, keepdims=True) + 1e-05)
    return inverse, (start * inverse * gain).astype(BF16)


def query_kernel(
    state_ref,
    cot_ref,
    encoder_t,
    decoder,
    gain_ref,
    query_t,
    output,
    start_ref,
    inverse_ref,
    top_ref,
    q_ref,
    qt_ref,
    g_ref,
    gt_ref,
):
    high, low = split(state_ref[...])
    start = dot(encoder_t[...], high) + dot(encoder_t[...], low)
    start_ref[...] = start
    inverse, normed = norm_t(start, gain_ref[...])
    inverse_ref[...] = inverse
    queries = dot(query_t[...], normed).astype(BF16)
    qt_ref[...] = queries
    q_ref[...] = queries.T
    high, low = split(cot_ref[...])
    top = dot(decoder[...], high) + dot(decoder[...], low)
    top_ref[...] = top
    grad = dot(output[...], top.astype(BF16)).astype(BF16)
    gt_ref[...] = grad
    g_ref[...] = grad.T


def attend_kernel(
    pattern,
    s0_ref,
    s1_ref,
    s2_ref,
    s3_ref,
    start_ref,
    inverse_ref,
    top_ref,
    q_ref,
    qt_ref,
    g_ref,
    gt_ref,
    encoder,
    encoder_t,
    gain_ref,
    query_w,
    key_w,
    value_w,
    key_t,
    value_t,
    output_t,
    decoder_t,
    decoded_ref,
    own_ref,
    o1_ref,
    o2_ref,
    o3_ref,
    enc_ref,
    start_s,
    inverse_s,
    keys_s,
    values_s,
    weight_s,
    prob_s,
    score_s,
    mixed_s,
    query_s,
    keyg_s,
    valueg_s,
):
    node_count = s0_ref.shape[1]
    pieces = (s0_ref, s1_ref, s2_ref, s3_ref)
    key_count = len(pieces) * node_count
    gain = gain_ref[...]
    scale = 1.0 / math.sqrt(HEAD)
    for r, piece in enumerate(pieces):
        span = pl.ds(r * node_count, node_count)
        start = dot(encoder_t[...], piece[...])
        start_s[:, span] = start
        inverse, normed = norm_t(start, gain)
        inverse_s[:, span] = inverse
        keys_s[:, span] = dot(key_t[...], normed).astype(BF16)
        values_s[:, span] = dot(value_t[...], normed).astype(BF16)

    def head(h, _):
        rows = pl.ds(pl.multiple_of(h * HEAD, HEAD), HEAD)
        q = q_ref[:, rows]
        g = g_ref[:, rows]
        kt = keys_s[rows, :]
        vt = values_s[rows, :]
        scores = dot(q, kt)
        for qt in range(node_count // TILE):
            for kb in range(key_count // TILE):
                bias = jnp.where(pattern[qt, kb] > 0, 0.0, -1e30).astype(F32)
                at = (slice(qt * TILE, (qt + 1) * TILE), slice(kb * TILE, (kb + 1) * TILE))
                weight_s[at] = scores[at] * (scale / math.log(2.0)) + bias
        biased = weight_s[...]
        weights = jnp.exp2(biased - jnp.max(biased, axis=1, keepdims=True))
        probs = weights * (1.0 / jnp.sum(weights, axis=1, keepdims=True))
        weight_s[...] = probs
        prob_s[...] = probs.astype(BF16)
        mixed = dot_nt(prob_s[...], vt)
        mixed_s[rows, :] = mixed.astype(BF16).T
        delta = jnp.sum(mixed * g.astype(F32), axis=1, keepdims=True)
        prob_grad = dot(g, vt)
        score_s[...] = (weight_s[...] * ((prob_grad - delta) * scale)).astype(BF16)
        query_s[rows, :] = dot_nt(score_s[...], kt).astype(BF16).T
        keyg_s[rows, :] = dot(qt_ref[rows, :], score_s[...]).astype(BF16)
        valueg_s[rows, :] = dot(gt_ref[rows, :], prob_s[...]).astype(BF16)
        return 0

    lax.fori_loop(0, HEADS, head, 0)
    final = start_ref[...] + dot(output_t[...], mixed_s[...])
    decoded_ref[...] = dot(decoder_t[...], final.astype(BF16)).astype(BF16)
    enc = jnp.zeros(enc_ref.shape, F32)
    for r, (piece, out) in enumerate(zip(pieces, (own_ref, o1_ref, o2_ref, o3_ref))):
        span = pl.ds(r * node_count, node_count)
        grad = dot(key_w[...], keyg_s[:, span]) + dot(value_w[...], valueg_s[:, span])
        if r == 0:
            grad = grad + dot(query_w[...], query_s[...])
            start, inverse = start_ref[...], inverse_ref[...]
        else:
            start, inverse = start_s[:, span], inverse_s[:, span]
        scaled = grad * gain
        mean = jnp.mean(start * scaled, axis=0, keepdims=True)
        total = inverse * scaled - start * (inverse * inverse * inverse * mean)
        if r == 0:
            total = total + top_ref[...]
        total = total.astype(BF16)
        out[...] = dot(encoder[...], total).astype(out.dtype)
        enc = enc + dot_nt(piece[...], total)
    enc_ref[...] = enc


def slots_kernel(own_idx, dec_idx, decoded_ref, own_ref, i1_ref, i2_ref, i3_ref, out_ref, grad_s):
    peers = out_ref.shape[0]
    node_count = decoded_ref.shape[1]
    total = own_ref[...]
    for piece in (i1_ref, i2_ref, i3_ref):
        total = total + piece[...].astype(F32)
    grad_s[...] = total.astype(BF16)
    nodes = lax.broadcasted_iota(jnp.int32, (node_count, TILE), 0)

    def step(pair, _):
        for k, index, data in ((0, dec_idx, decoded_ref), (1, own_idx, grad_s)):
            picks = [
                jnp.where(nodes == index[pl.ds(2 * pair + one, 1), :], 1.0, 0.0).astype(BF16)
                for one in range(2)
            ]
            got = dot(data[...], jnp.concatenate(picks, axis=1)).astype(BF16)
            out_ref[2 * pair, pl.ds(k * ROWS, ROWS), :] = got[:, :TILE]
            out_ref[2 * pair + 1, pl.ds(k * ROWS, ROWS), :] = got[:, TILE:]
        return 0

    lax.fori_loop(0, peers // 2, step, 0)


def unpack_kernel(back_ref, own_rank, dec_rank, denoised_ref, grad_ref, acc_d, acc_o):
    peers = back_ref.shape[0]
    variables = denoised_ref.shape[0]
    acc_d[...] = jnp.zeros_like(acc_d)
    acc_o[...] = jnp.zeros_like(acc_o)

    def step(pair, _):
        for k, rank, acc in ((0, dec_rank, acc_d), (1, own_rank, acc_o)):
            rows = pl.ds(k * ROWS, ROWS)
            data = jnp.concatenate([back_ref[2 * pair, rows, :], back_ref[2 * pair + 1, rows, :]], axis=1)
            acc[...] += dot(data, slot_onehot(rank, pair))
        return 0

    lax.fori_loop(0, peers // 2, step, 0)
    denoised_ref[...] = acc_d[0:variables, :].astype(BF16)
    grad_ref[...] = acc_o[0:variables, :]


def body(
    grid_state,
    cotangent,
    encoder_weight,
    norm_gain,
    query_weight,
    key_weight,
    value_weight,
    output_weight,
    decoder_weight,
    grid_owner,
    decode_node,
    tile_pattern,
):
    peers = lax.axis_size("wide")
    group = lax.axis_size("patch")
    variables, grid_count = grid_state.shape
    width = query_weight.shape[0]
    nodes = tile_pattern.shape[0] * TILE
    keys = group * nodes
    capacity = 2 * grid_count // peers
    shift = (nodes * group).bit_length() - 1
    vm = pltpu.VMEM

    send, own_rank, dec_rank = call(
        functools.partial(pack_kernel, shift),
        [((peers, 2 * ROWS, capacity), BF16), ((peers, grid_count), F32), ((peers, grid_count), F32)],
        [vm((ROWS, grid_count), F32), vm((ROWS, grid_count), BF16), vm((ROWS, grid_count), BF16)],
        "pack",
        4 * ROWS * grid_count * peers * capacity,
        grid_state,
        cotangent,
        grid_owner.reshape(1, grid_count),
        decode_node.reshape(1, grid_count),
    )
    recv = lax.all_to_all(send, "wide", split_axis=0, concat_axis=0, tiled=True)

    pad = ROWS - variables
    encoder = jnp.pad(encoder_weight, ((0, pad), (0, 0)))
    decoder = jnp.pad(decoder_weight, ((0, 0), (0, pad)))
    gain = norm_gain.astype(F32).reshape(width, 1)
    me = lax.axis_index("patch")
    pattern = jnp.roll(tile_pattern, -me * (nodes // TILE), axis=1)

    state, state_bf, cot, own_idx, dec_idx = call(
        functools.partial(sums_kernel, variables),
        [
            ((ROWS, nodes), F32),
            ((ROWS, nodes), BF16),
            ((ROWS, nodes), F32),
            ((peers, capacity), jnp.int32),
            ((peers, capacity), jnp.int32),
        ],
        [],
        "sums",
        4 * ROWS * nodes * peers * capacity,
        recv,
    )

    def from_ahead(x, r):
        return lax.ppermute(x, "patch", [((i + r) % group, i) for i in range(group)])

    def to_ahead(x, r):
        return lax.ppermute(x, "patch", [(i, (i + r) % group) for i in range(group)])

    pieces = [state_bf] + [from_ahead(state_bf, r) for r in range(1, group)]

    start, inverse, top, q, qt, g, gt = call(
        query_kernel,
        [
            ((width, nodes), F32),
            ((1, nodes), F32),
            ((width, nodes), F32),
            ((nodes, width), BF16),
            ((width, nodes), BF16),
            ((nodes, width), BF16),
            ((width, nodes), BF16),
        ],
        [],
        "query",
        4 * width * width * nodes,
        state,
        cot,
        encoder.T,
        decoder,
        gain,
        query_weight.T,
        output_weight,
    )
    decoded, own, o1, o2, o3, enc = call(
        attend_kernel,
        [((ROWS, nodes), BF16), ((ROWS, nodes), F32)]
        + [((ROWS, nodes), BF16)] * 3
        + [((ROWS, width), F32)],
        [
            vm((width, keys), F32),
            vm((1, keys), F32),
            vm((width, keys), BF16),
            vm((width, keys), BF16),
            vm((nodes, keys), F32),
            vm((nodes, keys), BF16),
            vm((nodes, keys), BF16),
            vm((width, nodes), BF16),
            vm((width, nodes), BF16),
            vm((width, keys), BF16),
            vm((width, keys), BF16),
        ],
        "attend",
        20 * nodes * keys * width,
        pattern,
        *pieces,
        start,
        inverse,
        top,
        q,
        qt,
        g,
        gt,
        encoder,
        encoder.T,
        gain,
        query_weight,
        key_weight,
        value_weight,
        key_weight.T,
        value_weight.T,
        output_weight.T,
        decoder.T,
        smem=(0,),
    )
    back = [to_ahead(o, r) for r, o in ((1, o1), (2, o2), (3, o3))]
    (reply,) = call(
        slots_kernel,
        [((peers, 2 * ROWS, capacity), BF16)],
        [vm((ROWS, nodes), BF16)],
        "slots",
        4 * ROWS * nodes * peers * capacity,
        own_idx,
        dec_idx,
        decoded,
        own,
        *back,
    )
    returned = lax.all_to_all(reply, "wide", split_axis=0, concat_axis=0, tiled=True)

    part = width // group
    turned = jnp.roll(enc, -me * part, axis=1)
    mine = turned[:, :part]
    for r in range(1, group):
        mine = mine + to_ahead(turned[:, r * part : (r + 1) * part], r)
    step = 1
    while step < peers:
        mine = mine + lax.ppermute(mine, "wide", [(i, i ^ step) for i in range(peers)])
        step *= 2
    whole = jnp.concatenate([mine] + [from_ahead(mine, r) for r in range(1, group)], axis=1)
    encoder_grad = jnp.roll(whole, me * part, axis=1)[:variables]

    denoised, state_grad = call(
        unpack_kernel,
        [((variables, grid_count), BF16), ((variables, grid_count), F32)],
        [vm((ROWS, grid_count), F32), vm((ROWS, grid_count), F32)],
        "unpack",
        4 * ROWS * grid_count * peers * capacity,
        returned,
        own_rank,
        dec_rank,
    )
    return (denoised, state_grad, encoder_grad)


def solution(mesh):
    in_specs = (
        P(None, ("wide", "patch")),
        P(None, ("wide", "patch")),
        P(),
        P(),
        P(),
        P(),
        P(),
        P(),
        P(),
        P(("wide", "patch")),
        P(("wide", "patch")),
        P(("wide", "patch"), None),
    )
    out_specs = (P(None, ("wide", "patch")), P(None, ("wide", "patch")), P())
    return jax.shard_map(body, mesh=mesh, in_specs=in_specs, out_specs=out_specs, check_vma=False)
```

```python
import functools
import math

import jax
import jax.numpy as jnp
from jax import lax
from jax.experimental import pallas as pl
from jax.experimental.pallas import tpu as pltpu
from jax.sharding import PartitionSpec as P

HEADS = 4
HEAD = 128
TILE = 128
ROWS = 88
F32 = jnp.float32
BF16 = jnp.bfloat16
MIB = 1024 * 1024
ATTEND_LIMIT = 28
SHARE = 11


def dot(a, b):
    return jnp.dot(a, b, preferred_element_type=F32)


def dot_nt(a, b):
    return lax.dot_general(a, b, (((1,), (1,)), ((), ())), preferred_element_type=F32)


def split(x):
    high = x.astype(BF16)
    return high, (x - high.astype(F32)).astype(BF16)


def call(kernel, outs, scratch, name, flops, *args, smem=(), limit=12):
    specs = [
        pl.BlockSpec(memory_space=pltpu.SMEM if i in smem else pltpu.VMEM) for i in range(len(args))
    ]
    return pl.pallas_call(
        kernel,
        out_shape=[jax.ShapeDtypeStruct(s, d) for s, d in outs],
        in_specs=specs,
        out_specs=[pl.BlockSpec(memory_space=pltpu.VMEM) for _ in outs],
        scratch_shapes=scratch,
        compiler_params=pltpu.CompilerParams(vmem_limit_bytes=limit * MIB),
        cost_estimate=pl.CostEstimate(flops=flops, bytes_accessed=1 << 20, transcendentals=0),
        name=name,
    )(*args)


def slot_onehot(rank_ref, pair):
    grid_count = rank_ref.shape[1]
    level = lax.broadcasted_iota(jnp.int32, (TILE, grid_count), 0).astype(F32).astype(BF16)
    parts = []
    for k in range(2):
        row = rank_ref[pl.ds(2 * pair + k, 1), :].astype(BF16)
        parts.append(jnp.where(level == row, jnp.ones((), BF16), jnp.zeros((), BF16)))
    return jnp.concatenate(parts, axis=0)


def loop(count, unroll, step):
    def some(i, _):
        for k in range(unroll):
            step(i * unroll + k)
        return 0

    lax.fori_loop(0, count // unroll, some, 0)


def pack_kernel(shift, mask, x_ref, index, out_ref, rank, wide_s, pay):
    variables, grid_count = x_ref.shape
    peers = out_ref.shape[0]
    chunk = 256
    upper = jnp.where(
        lax.broadcasted_iota(jnp.int32, (chunk, chunk), 0)
        < lax.broadcasted_iota(jnp.int32, (chunk, chunk), 1),
        1.0,
        0.0,
    ).astype(BF16)
    carry = jnp.zeros((peers, 1), F32)
    for start in range(0, grid_count, chunk):
        span = pl.ds(start, chunk)
        nodes = index[:, span]
        hit = lax.broadcasted_iota(jnp.int32, (peers, chunk), 0) == (nodes >> shift)
        ones = jnp.where(hit, 1.0, 0.0)
        before = dot(ones.astype(BF16), upper) + carry
        rank[:, span] = jnp.where(hit, before, -1.0)
        carry = carry + jnp.sum(ones, axis=1, keepdims=True)
    local = index[...] & mask
    wide_s[0:variables, :] = x_ref[...].astype(F32)
    wide_s[variables : variables + 1, :] = (local >> 1).astype(F32)
    wide_s[variables + 1 : variables + 2, :] = (local & 1).astype(F32)
    wide_s[variables + 2 : ROWS, :] = jnp.zeros((ROWS - variables - 2, grid_count), F32)
    pay[...] = wide_s[...].astype(BF16)

    def step(pair):
        got = dot_nt(pay[...], slot_onehot(rank, pair)).astype(BF16)
        out_ref[2 * pair] = got[:, :TILE]
        out_ref[2 * pair + 1] = got[:, TILE:]

    loop(peers // 2, 4, step)


def sums_kernel(variables, recv_ref, high_ref, low_ref, index, total_ref):
    peers = recv_ref.shape[0]
    node_count = total_ref.shape[1]
    nodes = lax.broadcasted_iota(jnp.int32, (node_count, TILE), 0)
    total_ref[...] = jnp.zeros_like(total_ref)

    def step(pair):
        data, picks = [], []
        for one in range(2):
            block = recv_ref[2 * pair + one]
            wide = block[80:ROWS].astype(F32)
            at = variables - 80
            slots = (2.0 * wide[at : at + 1] + wide[at + 1 : at + 2]).astype(jnp.int32)
            index[pl.ds(2 * pair + one, 1), :] = slots
            picks.append(jnp.where(nodes == slots, 1.0, 0.0).astype(BF16))
            data.append(block)
        total_ref[...] += dot_nt(jnp.concatenate(data, axis=1), jnp.concatenate(picks, axis=1))

    loop(peers // 2, 4, step)
    keep = lax.broadcasted_iota(jnp.int32, total_ref.shape, 0) < variables
    high_ref[...], low_ref[...] = split(jnp.where(keep, total_ref[...], 0.0))


def padded(ref, rows_s):
    rows_s[...] = jnp.zeros_like(rows_s)
    rows_s[0 : ref.shape[0], :] = ref[...].astype(F32)
    return rows_s[0:ROWS, :].astype(BF16), rows_s[...].T[:, :ROWS].astype(BF16)


def column(ref):
    return jnp.broadcast_to(ref[...].astype(F32), (TILE, ref.shape[1])).T[:, :1]


def norm_t(start, gain):
    inverse = lax.rsqrt(jnp.mean(start * start, axis=0, keepdims=True) + 1e-05)
    return inverse, (start * inverse * gain).astype(BF16)


def query_kernel(high, low, enc, gain_ref, query_w, start_ref, inverse_ref, q_ref, qt_ref, rows_s):
    _, encoder_t = padded(enc, rows_s)
    start = dot(encoder_t, high[...]) + dot(encoder_t, low[...])
    start_ref[...] = start
    inverse, normed = norm_t(start, column(gain_ref))
    inverse_ref[...] = inverse
    queries = dot(query_w[...].T, normed).astype(BF16)
    qt_ref[...] = queries
    q_ref[...] = queries.T


def top_kernel(high, low, dec, output, top_ref, g_ref, gt_ref, rows_s):
    _, decoder = padded(dec, rows_s)
    top = dot(decoder, high[...]) + dot(decoder, low[...])
    top_ref[...] = top
    grad = dot(output[...], top.astype(BF16)).astype(BF16)
    gt_ref[...] = grad
    g_ref[...] = grad.T


def attend_kernel(
    place,
    pattern,
    s0_ref,
    s1_ref,
    s2_ref,
    s3_ref,
    start_ref,
    inverse_ref,
    top_ref,
    q_ref,
    qt_ref,
    g_ref,
    gt_ref,
    enc,
    gain_ref,
    query_w,
    key_w,
    value_w,
    output_w,
    dec,
    decoded_ref,
    own_ref,
    o1_ref,
    o2_ref,
    o3_ref,
    enc_ref,
    start_s,
    inverse_s,
    keys_s,
    values_s,
    weight_s,
    prob_s,
    score_s,
    mixed_s,
    query_s,
    keyg_s,
    valueg_s,
    rows_s,
):
    node_count = s0_ref.shape[1]
    pieces = (s0_ref, s1_ref, s2_ref, s3_ref)
    key_tiles = len(pieces) * node_count // TILE
    gain = column(gain_ref)
    _, encoder_t = padded(enc, rows_s)
    key_t = key_w[...].T
    value_t = value_w[...].T
    scale = 1.0 / math.sqrt(HEAD)
    for r, piece in enumerate(pieces):
        span = pl.ds(r * node_count, node_count)
        start = dot(encoder_t, piece[...])
        start_s[:, span] = start
        inverse, normed = norm_t(start, gain)
        inverse_s[:, span] = inverse
        keys_s[:, span] = dot(key_t, normed).astype(BF16)
        values_s[:, span] = dot(value_t, normed).astype(BF16)
    first = place[0] * (node_count // TILE)

    def head(h, _):
        rows = pl.ds(pl.multiple_of(h * HEAD, HEAD), HEAD)
        g = g_ref[:, rows]
        kt = keys_s[rows, :]
        vt = values_s[rows, :]
        scores = dot(q_ref[:, rows], kt)
        for qt in range(node_count // TILE):
            for kb in range(key_tiles):
                seen = pattern[qt, lax.rem(first + kb, key_tiles)] > 0
                bias = jnp.where(seen, 0.0, -1e30).astype(F32)
                at = (slice(qt * TILE, (qt + 1) * TILE), slice(kb * TILE, (kb + 1) * TILE))
                weight_s[at] = scores[at] * (scale / math.log(2.0)) + bias
        biased = weight_s[...]
        weights = jnp.exp2(biased - jnp.max(biased, axis=1, keepdims=True))
        probs = weights * (1.0 / jnp.sum(weights, axis=1, keepdims=True))
        weight_s[...] = probs
        prob_s[...] = probs.astype(BF16)
        mixed = dot_nt(prob_s[...], vt)
        mixed_s[rows, :] = mixed.astype(BF16).T
        delta = jnp.sum(mixed * g.astype(F32), axis=1, keepdims=True)
        prob_grad = dot(g, vt)
        score_s[...] = (weight_s[...] * ((prob_grad - delta) * scale)).astype(BF16)
        query_s[rows, :] = dot_nt(score_s[...], kt).astype(BF16).T
        keyg_s[rows, :] = dot(qt_ref[rows, :], score_s[...]).astype(BF16)
        valueg_s[rows, :] = dot(gt_ref[rows, :], prob_s[...]).astype(BF16)
        return 0

    lax.fori_loop(0, HEADS, head, 0)
    final = start_ref[...] + dot(output_w[...].T, mixed_s[...])
    decoder_t, _ = padded(dec, rows_s)
    decoded_ref[...] = dot(decoder_t, final.astype(BF16)).astype(BF16)
    encoder, _ = padded(enc, rows_s)
    total_enc = jnp.zeros(enc_ref.shape, F32)
    for r, (piece, out) in enumerate(zip(pieces, (own_ref, o1_ref, o2_ref, o3_ref))):
        span = pl.ds(r * node_count, node_count)
        grad = dot(key_w[...], keyg_s[:, span]) + dot(value_w[...], valueg_s[:, span])
        if r == 0:
            grad = grad + dot(query_w[...], query_s[...])
            start, inverse = start_ref[...], inverse_ref[...]
        else:
            start, inverse = start_s[:, span], inverse_s[:, span]
        scaled = grad * gain
        mean = jnp.mean(start * scaled, axis=0, keepdims=True)
        total = inverse * scaled - start * (inverse * inverse * inverse * mean)
        if r == 0:
            total = total + top_ref[...]
        total = total.astype(BF16)
        out[...] = dot(encoder, total).astype(out.dtype)
        total_enc = total_enc + dot_nt(piece[...], total)
    enc_ref[...] = total_enc


def picks_of(index, pair, nodes):
    return jnp.concatenate(
        [
            jnp.where(nodes == index[pl.ds(2 * pair + one, 1), :], 1.0, 0.0).astype(BF16)
            for one in range(2)
        ],
        axis=1,
    )


def decoded_slots_kernel(index, decoded_ref, enc_ref, out_ref, whole, extra):
    peers = out_ref.shape[0]
    height = enc_ref.shape[0]
    for t in range(enc_ref.shape[1] // TILE):
        whole[t * height : (t + 1) * height, :] = enc_ref[:, t * TILE : (t + 1) * TILE]
    extra[...] = jnp.zeros_like(extra)
    for j in range(SHARE):
        rows = whole[j * peers : (j + 1) * peers, :]
        high = rows.astype(BF16).astype(F32)
        extra[pl.ds(j, peers, stride=24), :] = high
        extra[pl.ds(SHARE + j, peers, stride=24), :] = rows - high
    nodes = lax.broadcasted_iota(jnp.int32, (decoded_ref.shape[1], TILE), 0)

    def step(pair):
        got = dot(decoded_ref[...], picks_of(index, pair, nodes))
        for one in range(2):
            tail = extra[pl.ds(pl.multiple_of((2 * pair + one) * 24, 8), 24), :]
            rows = jnp.concatenate([got[:, one * TILE : (one + 1) * TILE], tail], axis=0)
            out_ref[2 * pair + one] = rows.astype(BF16)

    loop(peers // 2, 4, step)


def grad_slots_kernel(index, own_ref, i1_ref, i2_ref, i3_ref, out_ref, grad_s):
    total = own_ref[...]
    for piece in (i1_ref, i2_ref, i3_ref):
        total = total + piece[...].astype(F32)
    grad_s[...] = total.astype(BF16)
    nodes = lax.broadcasted_iota(jnp.int32, (own_ref.shape[1], TILE), 0)
    blank = jnp.zeros((out_ref.shape[1] - ROWS, TILE), F32)

    def step(pair):
        got = dot(grad_s[...], picks_of(index, pair, nodes))
        for one in range(2):
            rows = jnp.concatenate([got[:, one * TILE : (one + 1) * TILE], blank], axis=0)
            out_ref[2 * pair + one] = rows.astype(BF16)

    loop(out_ref.shape[0] // 2, 4, step)


def unpack_kernel(back_ref, rank, out_ref, acc):
    peers = back_ref.shape[0]
    acc[...] = jnp.zeros_like(acc)

    def step(pair):
        data = jnp.concatenate([back_ref[2 * pair], back_ref[2 * pair + 1]], axis=1)
        acc[...] += dot(data[:ROWS], slot_onehot(rank, pair))

    loop(peers // 2, 4, step)
    out_ref[...] = acc[0 : out_ref.shape[0], :].astype(out_ref.dtype)


def body(
    grid_state,
    cotangent,
    encoder_weight,
    norm_gain,
    query_weight,
    key_weight,
    value_weight,
    output_weight,
    decoder_weight,
    grid_owner,
    decode_node,
    tile_pattern,
):
    peers = lax.axis_size("wide")
    group = lax.axis_size("patch")
    variables, grid_count = grid_state.shape
    width = query_weight.shape[0]
    nodes = tile_pattern.shape[0] * TILE
    keys = group * nodes
    capacity = 2 * grid_count // peers
    shift = (nodes * group).bit_length() - 1
    vm = pltpu.VMEM

    route = 2 * ROWS * grid_count * peers * capacity
    spread = 2 * ROWS * nodes * peers * capacity

    def exchange(x):
        return lax.all_to_all(x, "wide", split_axis=0, concat_axis=0, tiled=True)

    def pack(x, index):
        return call(
            functools.partial(pack_kernel, shift, nodes - 1),
            [((peers, ROWS, capacity), BF16), ((peers, grid_count), F32)],
            [vm((ROWS, grid_count), F32), vm((ROWS, grid_count), BF16)],
            "pack",
            route,
            x,
            index.reshape(1, grid_count),
        )

    def sums(recv):
        return call(
            functools.partial(sums_kernel, variables),
            [((ROWS, nodes), BF16), ((ROWS, nodes), BF16), ((peers, capacity), jnp.int32)],
            [vm((ROWS, nodes), F32)],
            "sums",
            spread,
            recv,
        )

    def unpack(x, rank, dtype):
        return call(
            unpack_kernel,
            [((variables, grid_count), dtype)],
            [vm((ROWS, grid_count), F32)],
            "unpack",
            route,
            x,
            rank,
        )[0]

    def from_ahead(x, r):
        return lax.ppermute(x, "patch", [((i + r) % group, i) for i in range(group)])

    def to_ahead(x, r):
        return lax.ppermute(x, "patch", [(i, (i + r) % group) for i in range(group)])

    place = lax.axis_index("patch").reshape(1).astype(jnp.int32)
    gain = norm_gain.reshape(1, width)
    decoder_rows = decoder_weight.T

    state_send, own_rank = pack(grid_state, grid_owner)
    cotangent, state_send = lax.optimization_barrier((cotangent, state_send))
    state_recv = exchange(state_send)
    cot_send, dec_rank = pack(cotangent, decode_node)
    cot_recv = exchange(cot_send)

    state, state_low, own_idx = sums(state_recv)
    pieces = [state] + [from_ahead(state, r) for r in range(1, group)]
    square = ((width, nodes), BF16)
    start, inverse, q, qt = call(
        query_kernel,
        [((width, nodes), F32), ((1, nodes), F32), square, square],
        [vm((TILE, width), F32)],
        "query",
        3 * width * width * nodes,
        state,
        state_low,
        encoder_weight,
        gain,
        query_weight,
    )
    cot, cot_low, dec_idx = sums(cot_recv)
    top, g, gt = call(
        top_kernel,
        [((width, nodes), F32), square, square],
        [vm((TILE, width), F32)],
        "top",
        3 * width * width * nodes,
        cot,
        cot_low,
        decoder_rows,
        output_weight,
    )
    decoded, own, o1, o2, o3, enc = call(
        attend_kernel,
        [((ROWS, nodes), BF16), ((ROWS, nodes), F32)]
        + [((ROWS, nodes), BF16)] * 3
        + [((ROWS, width), F32)],
        [
            vm((width, keys), F32),
            vm((1, keys), F32),
            vm((width, keys), BF16),
            vm((width, keys), BF16),
            vm((nodes, keys), F32),
            vm((nodes, keys), BF16),
            vm((nodes, keys), BF16),
            vm((width, nodes), BF16),
            vm((width, nodes), BF16),
            vm((width, keys), BF16),
            vm((width, keys), BF16),
            vm((TILE, width), F32),
        ],
        "attend",
        20 * nodes * keys * width,
        place,
        tile_pattern,
        *pieces,
        start,
        inverse,
        top,
        q,
        qt,
        g,
        gt,
        encoder_weight,
        gain,
        query_weight,
        key_weight,
        value_weight,
        output_weight,
        decoder_rows,
        smem=(0, 1),
        limit=ATTEND_LIMIT,
    )
    back = [to_ahead(o, r) for r, o in ((1, o1), (2, o2), (3, o3))]
    (decoded_send,) = call(
        decoded_slots_kernel,
        [((peers, ROWS + 24, capacity), BF16)],
        [vm((peers * SHARE, TILE), F32), vm((peers * 24, TILE), F32)],
        "decoded_slots",
        spread,
        dec_idx,
        decoded,
        enc,
    )
    decoded_back = exchange(decoded_send)
    (grad_send,) = call(
        grad_slots_kernel,
        [((peers, ROWS + 8, capacity), BF16)],
        [vm((ROWS, nodes), BF16)],
        "grad_slots",
        spread,
        own_idx,
        own,
        *back,
    )
    chunk = jnp.sum(decoded_back[:, ROWS : ROWS + 2 * SHARE].astype(F32), axis=0)
    chunk = (chunk[:SHARE] + chunk[SHARE:]).astype(BF16)
    span = slice(variables, variables + SHARE)
    grad_send = grad_send.at[:, span].set(jnp.broadcast_to(chunk, (peers,) + chunk.shape))
    grad_back = exchange(grad_send)
    denoised = unpack(decoded_back, dec_rank, BF16)
    grad_back, denoised = lax.optimization_barrier((grad_back, denoised))
    mine = jnp.swapaxes(grad_back[:, span], 0, 1).reshape(peers * SHARE, TILE)
    parts = [mine] + [from_ahead(mine, r) for r in range(1, group)]
    state_grad = unpack(grad_back, own_rank, F32)
    whole = sum(p.astype(F32) for p in parts).reshape(width // TILE, ROWS, TILE)
    encoder_grad = jnp.swapaxes(whole, 0, 1).reshape(ROWS, width)[:variables]
    return (denoised, state_grad, encoder_grad)


def solution(mesh):
    in_specs = (
        P(None, ("wide", "patch")),
        P(None, ("wide", "patch")),
        P(),
        P(),
        P(),
        P(),
        P(),
        P(),
        P(),
        P(("wide", "patch")),
        P(("wide", "patch")),
        P(("wide", "patch"), None),
    )
    out_specs = (P(None, ("wide", "patch")), P(None, ("wide", "patch")), P())
    return jax.shard_map(body, mesh=mesh, in_specs=in_specs, out_specs=out_specs, check_vma=False)
```

```python
import functools
import math

import jax
import jax.numpy as jnp
from jax import lax
from jax.experimental import pallas as pl
from jax.experimental.pallas import tpu as pltpu
from jax.sharding import PartitionSpec as P

HEADS = 4
HEAD = 128
TILE = 128
ROWS = 88
F32 = jnp.float32
BF16 = jnp.bfloat16
MIB = 1024 * 1024
ATTEND_LIMIT = 38
SHARE = 11


def dot(a, b):
    return jnp.dot(a, b, preferred_element_type=F32)


def dot_nt(a, b):
    return lax.dot_general(a, b, (((1,), (1,)), ((), ())), preferred_element_type=F32)


def split(x):
    high = x.astype(BF16)
    return high, (x - high.astype(F32)).astype(BF16)


def call(kernel, outs, scratch, name, flops, *args, smem=(), limit=12):
    specs = [
        pl.BlockSpec(memory_space=pltpu.SMEM if i in smem else pltpu.VMEM) for i in range(len(args))
    ]
    return pl.pallas_call(
        kernel,
        out_shape=[jax.ShapeDtypeStruct(s, d) for s, d in outs],
        in_specs=specs,
        out_specs=[pl.BlockSpec(memory_space=pltpu.VMEM) for _ in outs],
        scratch_shapes=scratch,
        compiler_params=pltpu.CompilerParams(vmem_limit_bytes=limit * MIB),
        cost_estimate=pl.CostEstimate(flops=flops, bytes_accessed=1 << 20, transcendentals=0),
        name=name,
    )(*args)


def slot_targets(route):
    level = lax.broadcasted_iota(jnp.int32, (TILE, route.shape[1]), 0).astype(F32).astype(BF16)
    rank, target = route[0:1, :].astype(BF16), route[1:2, :].astype(BF16)
    return jnp.where(level == rank, target, jnp.full((), -1.0, BF16))


def slot_onehot(targets, pair, axis):
    parts = []
    for k in range(2):
        peer = (jnp.zeros((1, targets.shape[1]), F32) + (2 * pair + k).astype(F32)).astype(BF16)
        parts.append(jnp.where(targets[...] == peer, jnp.ones((), BF16), jnp.zeros((), BF16)))
    return jnp.concatenate(parts, axis=axis)


def loop(count, unroll, step):
    def some(i, _):
        for k in range(unroll):
            step(i * unroll + k)
        return 0

    lax.fori_loop(0, count // unroll, some, 0)


def pack_kernel(shift, mask, x_ref, index, out_ref, route, wide_s, pay, targets):
    variables, grid_count = x_ref.shape
    peers = out_ref.shape[0]
    chunk = 256
    upper = jnp.where(
        lax.broadcasted_iota(jnp.int32, (chunk, chunk), 0)
        < lax.broadcasted_iota(jnp.int32, (chunk, chunk), 1),
        1.0,
        0.0,
    ).astype(BF16)
    carry = jnp.zeros((peers, 1), F32)
    for start in range(0, grid_count, chunk):
        span = pl.ds(start, chunk)
        nodes = index[:, span]
        hit = lax.broadcasted_iota(jnp.int32, (peers, chunk), 0) == (nodes >> shift)
        ones = jnp.where(hit, 1.0, 0.0)
        before = dot(ones.astype(BF16), upper) + carry
        route[0:1, span] = jnp.sum(jnp.where(hit, before, 0.0), axis=0, keepdims=True)
        route[1:2, span] = (nodes >> shift).astype(F32)
        carry = carry + jnp.sum(ones, axis=1, keepdims=True)
    local = index[...] & mask
    wide_s[0:variables, :] = x_ref[...].astype(F32)
    wide_s[variables : variables + 1, :] = (local >> 1).astype(F32)
    wide_s[variables + 1 : variables + 2, :] = (local & 1).astype(F32)
    wide_s[variables + 2 : ROWS, :] = jnp.zeros((ROWS - variables - 2, grid_count), F32)
    pay[...] = wide_s[...].astype(BF16)
    targets[...] = slot_targets(route).T

    def step(pair):
        got = dot(pay[...], slot_onehot(targets, pair, 1)).astype(BF16)
        out_ref[2 * pair] = got[:, :TILE]
        out_ref[2 * pair + 1] = got[:, TILE:]

    loop(peers // 2, 4, step)


def sums_kernel(variables, recv_ref, high_ref, low_ref, index, total_ref):
    peers = recv_ref.shape[0]
    node_count = total_ref.shape[1]
    nodes = lax.broadcasted_iota(jnp.int32, (node_count, TILE), 0)
    total_ref[...] = jnp.zeros_like(total_ref)

    def step(pair):
        data, picks = [], []
        for one in range(2):
            block = recv_ref[2 * pair + one]
            wide = block[80:ROWS].astype(F32)
            at = variables - 80
            slots = (2.0 * wide[at : at + 1] + wide[at + 1 : at + 2]).astype(jnp.int32)
            index[pl.ds(2 * pair + one, 1), :] = slots
            picks.append(jnp.where(nodes == slots, 1.0, 0.0).astype(BF16))
            data.append(block)
        total_ref[...] += dot_nt(jnp.concatenate(data, axis=1), jnp.concatenate(picks, axis=1))

    loop(peers // 2, 4, step)
    keep = lax.broadcasted_iota(jnp.int32, total_ref.shape, 0) < variables
    high_ref[...], low_ref[...] = split(jnp.where(keep, total_ref[...], 0.0))


def padded(ref, rows_s):
    rows_s[...] = jnp.zeros_like(rows_s)
    rows_s[0 : ref.shape[0], :] = ref[...].astype(F32)
    return rows_s[0:ROWS, :].astype(BF16), rows_s[...].T[:, :ROWS].astype(BF16)


def column(ref):
    return jnp.broadcast_to(ref[...].astype(F32), (TILE, ref.shape[1])).T[:, :1]


def norm_t(start, gain):
    inverse = lax.rsqrt(jnp.mean(start * start, axis=0, keepdims=True) + 1e-05)
    return inverse, (start * inverse * gain).astype(BF16)


def query_kernel(high, low, enc, gain_ref, query_w, start_ref, inverse_ref, q_ref, qt_ref, rows_s):
    _, encoder_t = padded(enc, rows_s)
    start = dot(encoder_t, high[...]) + dot(encoder_t, low[...])
    start_ref[...] = start
    inverse, normed = norm_t(start, column(gain_ref))
    inverse_ref[...] = inverse
    queries = dot(query_w[...].T, normed).astype(BF16)
    qt_ref[...] = queries
    q_ref[...] = queries.T


def top_kernel(high, low, dec, output, top_ref, g_ref, gt_ref, rows_s):
    _, decoder = padded(dec, rows_s)
    top = dot(decoder, high[...]) + dot(decoder, low[...])
    top_ref[...] = top
    grad = dot(output[...], top.astype(BF16)).astype(BF16)
    gt_ref[...] = grad
    g_ref[...] = grad.T


def attend_kernel(
    place,
    pattern,
    s0_ref,
    s1_ref,
    s2_ref,
    s3_ref,
    start_ref,
    inverse_ref,
    top_ref,
    q_ref,
    qt_ref,
    g_ref,
    gt_ref,
    enc,
    gain_ref,
    query_w,
    key_w,
    value_w,
    output_w,
    dec,
    decoded_ref,
    own_ref,
    o1_ref,
    o2_ref,
    o3_ref,
    enc_ref,
    start_s,
    inverse_s,
    keys_s,
    values_s,
    weight0_s,
    weight1_s,
    prob0_s,
    prob1_s,
    score0_s,
    score1_s,
    mixed_s,
    query_s,
    keyg_s,
    valueg_s,
    rows_s,
):
    node_count = s0_ref.shape[1]
    pieces = (s0_ref, s1_ref, s2_ref, s3_ref)
    key_tiles = len(pieces) * node_count // TILE
    gain = column(gain_ref)
    _, encoder_t = padded(enc, rows_s)
    key_t = key_w[...].T
    value_t = value_w[...].T
    scale = 1.0 / math.sqrt(HEAD)
    for r, piece in enumerate(pieces):
        span = pl.ds(r * node_count, node_count)
        start = dot(encoder_t, piece[...])
        start_s[:, span] = start
        inverse, normed = norm_t(start, gain)
        inverse_s[:, span] = inverse
        keys_s[:, span] = dot(key_t, normed).astype(BF16)
        values_s[:, span] = dot(value_t, normed).astype(BF16)
    first = place[0] * (node_count // TILE)

    weight_s = (weight0_s, weight1_s)
    prob_s = (prob0_s, prob1_s)
    score_s = (score0_s, score1_s)

    def soft(h):
        rows = pl.ds(h * HEAD, HEAD)
        weight, prob = weight_s[h % 2], prob_s[h % 2]
        scores = dot(q_ref[:, rows], keys_s[rows, :])
        for qt in range(node_count // TILE):
            for kb in range(key_tiles):
                seen = pattern[qt, lax.rem(first + kb, key_tiles)] > 0
                bias = jnp.where(seen, 0.0, -1e30).astype(F32)
                at = (slice(qt * TILE, (qt + 1) * TILE), slice(kb * TILE, (kb + 1) * TILE))
                weight[at] = scores[at] * (scale / math.log(2.0)) + bias
        biased = weight[...]
        weights = jnp.exp2(biased - jnp.max(biased, axis=1, keepdims=True))
        probs = weights * (1.0 / jnp.sum(weights, axis=1, keepdims=True))
        weight[...] = probs
        prob[...] = probs.astype(BF16)

    def rest(h):
        rows = pl.ds(h * HEAD, HEAD)
        weight, prob, score = weight_s[h % 2], prob_s[h % 2], score_s[h % 2]
        g, kt, vt = g_ref[:, rows], keys_s[rows, :], values_s[rows, :]
        mixed = dot_nt(prob[...], vt)
        mixed_s[rows, :] = mixed.astype(BF16).T
        delta = jnp.sum(mixed * g.astype(F32), axis=1, keepdims=True)
        prob_grad = dot(g, vt)
        score[...] = (weight[...] * ((prob_grad - delta) * scale)).astype(BF16)
        query_s[rows, :] = dot_nt(score[...], kt).astype(BF16).T
        keyg_s[rows, :] = dot(qt_ref[rows, :], score[...]).astype(BF16)
        valueg_s[rows, :] = dot(gt_ref[rows, :], prob[...]).astype(BF16)

    soft(0)
    for h in range(HEADS):
        if h + 1 < HEADS:
            soft(h + 1)
        rest(h)
    final = start_ref[...] + dot(output_w[...].T, mixed_s[...])
    decoder_t, _ = padded(dec, rows_s)
    decoded_ref[...] = dot(decoder_t, final.astype(BF16)).astype(BF16)
    encoder, _ = padded(enc, rows_s)
    total_enc = jnp.zeros(enc_ref.shape, F32)
    for r, (piece, out) in enumerate(zip(pieces, (own_ref, o1_ref, o2_ref, o3_ref))):
        span = pl.ds(r * node_count, node_count)
        grad = dot(key_w[...], keyg_s[:, span]) + dot(value_w[...], valueg_s[:, span])
        if r == 0:
            grad = grad + dot(query_w[...], query_s[...])
            start, inverse = start_ref[...], inverse_ref[...]
        else:
            start, inverse = start_s[:, span], inverse_s[:, span]
        scaled = grad * gain
        mean = jnp.mean(start * scaled, axis=0, keepdims=True)
        total = inverse * scaled - start * (inverse * inverse * inverse * mean)
        if r == 0:
            total = total + top_ref[...]
        total = total.astype(BF16)
        out[...] = dot(encoder, total).astype(out.dtype)
        total_enc = total_enc + dot_nt(piece[...], total)
    enc_ref[...] = total_enc


def picks_of(index, pair, nodes):
    return jnp.concatenate(
        [
            jnp.where(nodes == index[pl.ds(2 * pair + one, 1), :], 1.0, 0.0).astype(BF16)
            for one in range(2)
        ],
        axis=1,
    )


def decoded_slots_kernel(index, decoded_ref, enc_ref, out_ref, whole, extra):
    peers = out_ref.shape[0]
    height = enc_ref.shape[0]
    for t in range(enc_ref.shape[1] // TILE):
        whole[t * height : (t + 1) * height, :] = enc_ref[:, t * TILE : (t + 1) * TILE]
    extra[...] = jnp.zeros_like(extra)
    for j in range(SHARE):
        rows = whole[j * peers : (j + 1) * peers, :]
        high = rows.astype(BF16).astype(F32)
        extra[pl.ds(j, peers, stride=24), :] = high
        extra[pl.ds(SHARE + j, peers, stride=24), :] = rows - high
    nodes = lax.broadcasted_iota(jnp.int32, (decoded_ref.shape[1], TILE), 0)

    def step(pair):
        got = dot(decoded_ref[...], picks_of(index, pair, nodes))
        for one in range(2):
            tail = extra[pl.ds(pl.multiple_of((2 * pair + one) * 24, 8), 24), :]
            rows = jnp.concatenate([got[:, one * TILE : (one + 1) * TILE], tail], axis=0)
            out_ref[2 * pair + one] = rows.astype(BF16)

    loop(peers // 2, 4, step)


def grad_slots_kernel(index, own_ref, i1_ref, i2_ref, i3_ref, out_ref, grad_s):
    total = own_ref[...]
    for piece in (i1_ref, i2_ref, i3_ref):
        total = total + piece[...].astype(F32)
    grad_s[...] = total.astype(BF16)
    nodes = lax.broadcasted_iota(jnp.int32, (own_ref.shape[1], TILE), 0)
    blank = jnp.zeros((out_ref.shape[1] - ROWS, TILE), F32)

    def step(pair):
        got = dot(grad_s[...], picks_of(index, pair, nodes))
        for one in range(2):
            rows = jnp.concatenate([got[:, one * TILE : (one + 1) * TILE], blank], axis=0)
            out_ref[2 * pair + one] = rows.astype(BF16)

    loop(out_ref.shape[0] // 2, 4, step)


def unpack_kernel(back_ref, route, out_ref, acc, targets):
    peers = back_ref.shape[0]
    targets[...] = slot_targets(route)
    acc[...] = jnp.zeros_like(acc)

    def step(pair):
        data = jnp.concatenate([back_ref[2 * pair], back_ref[2 * pair + 1]], axis=1)
        acc[...] += dot(data[:ROWS], slot_onehot(targets, pair, 0))

    loop(peers // 2, 4, step)
    out_ref[...] = acc[0 : out_ref.shape[0], :].astype(out_ref.dtype)


def body(
    grid_state,
    cotangent,
    encoder_weight,
    norm_gain,
    query_weight,
    key_weight,
    value_weight,
    output_weight,
    decoder_weight,
    grid_owner,
    decode_node,
    tile_pattern,
):
    peers = lax.axis_size("wide")
    group = lax.axis_size("patch")
    variables, grid_count = grid_state.shape
    width = query_weight.shape[0]
    nodes = tile_pattern.shape[0] * TILE
    keys = group * nodes
    capacity = 2 * grid_count // peers
    shift = (nodes * group).bit_length() - 1
    vm = pltpu.VMEM

    route = 2 * ROWS * grid_count * peers * capacity
    spread = 2 * ROWS * nodes * peers * capacity

    def exchange(x):
        return lax.all_to_all(x, "wide", split_axis=0, concat_axis=0, tiled=True)

    def pack(x, index):
        return call(
            functools.partial(pack_kernel, shift, nodes - 1),
            [((peers, ROWS, capacity), BF16), ((2, grid_count), F32)],
            [
                vm((ROWS, grid_count), F32),
                vm((ROWS, grid_count), BF16),
                vm((grid_count, capacity), BF16),
            ],
            "pack",
            route,
            x,
            index.reshape(1, grid_count),
        )

    def sums(recv):
        return call(
            functools.partial(sums_kernel, variables),
            [((ROWS, nodes), BF16), ((ROWS, nodes), BF16), ((peers, capacity), jnp.int32)],
            [vm((ROWS, nodes), F32)],
            "sums",
            spread,
            recv,
        )

    def unpack(x, slots, dtype):
        return call(
            unpack_kernel,
            [((variables, grid_count), dtype)],
            [vm((ROWS, grid_count), F32), vm((capacity, grid_count), BF16)],
            "unpack",
            route,
            x,
            slots,
        )[0]

    def from_ahead(x, r):
        return lax.ppermute(x, "patch", [((i + r) % group, i) for i in range(group)])

    def to_ahead(x, r):
        return lax.ppermute(x, "patch", [(i, (i + r) % group) for i in range(group)])

    place = lax.axis_index("patch").reshape(1).astype(jnp.int32)
    gain = norm_gain.reshape(1, width)
    decoder_rows = decoder_weight.T

    state_send, own_slots = pack(grid_state, grid_owner)
    cotangent, state_send = lax.optimization_barrier((cotangent, state_send))
    state_recv = exchange(state_send)
    cot_send, dec_slots = pack(cotangent, decode_node)
    cot_recv = exchange(cot_send)

    state, state_low, own_idx = sums(state_recv)
    pieces = [state] + [from_ahead(state, r) for r in range(1, group)]
    square = ((width, nodes), BF16)
    start, inverse, q, qt = call(
        query_kernel,
        [((width, nodes), F32), ((1, nodes), F32), square, square],
        [vm((TILE, width), F32)],
        "query",
        3 * width * width * nodes,
        state,
        state_low,
        encoder_weight,
        gain,
        query_weight,
    )
    cot, cot_low, dec_idx = sums(cot_recv)
    top, g, gt = call(
        top_kernel,
        [((width, nodes), F32), square, square],
        [vm((TILE, width), F32)],
        "top",
        3 * width * width * nodes,
        cot,
        cot_low,
        decoder_rows,
        output_weight,
    )
    decoded, own, o1, o2, o3, enc = call(
        attend_kernel,
        [((ROWS, nodes), BF16), ((ROWS, nodes), F32)]
        + [((ROWS, nodes), BF16)] * 3
        + [((ROWS, width), F32)],
        [
            vm((width, keys), F32),
            vm((1, keys), F32),
            vm((width, keys), BF16),
            vm((width, keys), BF16),
            vm((nodes, keys), F32),
            vm((nodes, keys), F32),
            vm((nodes, keys), BF16),
            vm((nodes, keys), BF16),
            vm((nodes, keys), BF16),
            vm((nodes, keys), BF16),
            vm((width, nodes), BF16),
            vm((width, nodes), BF16),
            vm((width, keys), BF16),
            vm((width, keys), BF16),
            vm((TILE, width), F32),
        ],
        "attend",
        20 * nodes * keys * width,
        place,
        tile_pattern,
        *pieces,
        start,
        inverse,
        top,
        q,
        qt,
        g,
        gt,
        encoder_weight,
        gain,
        query_weight,
        key_weight,
        value_weight,
        output_weight,
        decoder_rows,
        smem=(0, 1),
        limit=ATTEND_LIMIT,
    )
    back = [to_ahead(o, r) for r, o in ((1, o1), (2, o2), (3, o3))]
    (decoded_send,) = call(
        decoded_slots_kernel,
        [((peers, ROWS + 24, capacity), BF16)],
        [vm((peers * SHARE, TILE), F32), vm((peers * 24, TILE), F32)],
        "decoded_slots",
        spread,
        dec_idx,
        decoded,
        enc,
    )
    decoded_back = exchange(decoded_send)
    (grad_send,) = call(
        grad_slots_kernel,
        [((peers, ROWS + 8, capacity), BF16)],
        [vm((ROWS, nodes), BF16)],
        "grad_slots",
        spread,
        own_idx,
        own,
        *back,
    )
    chunk = jnp.sum(decoded_back[:, ROWS : ROWS + 2 * SHARE].astype(F32), axis=0)
    chunk = (chunk[:SHARE] + chunk[SHARE:]).astype(BF16)
    span = slice(variables, variables + SHARE)
    chunk = jnp.broadcast_to(chunk, (peers,) + chunk.shape)
    grad_send = lax.dynamic_update_slice(grad_send, chunk, (0, variables, 0))
    grad_back = exchange(grad_send)
    denoised = unpack(decoded_back, dec_slots, BF16)
    grad_back, denoised = lax.optimization_barrier((grad_back, denoised))
    mine = jnp.swapaxes(grad_back[:, span], 0, 1).reshape(peers * SHARE, TILE)
    parts = [mine] + [from_ahead(mine, r) for r in range(1, group)]
    state_grad = unpack(grad_back, own_slots, F32)
    whole = sum(p.astype(F32) for p in parts).reshape(width // TILE, ROWS, TILE)
    encoder_grad = jnp.swapaxes(whole, 0, 1).reshape(ROWS, width)[:variables]
    return (denoised, state_grad, encoder_grad)


def solution(mesh):
    in_specs = (
        P(None, ("wide", "patch")),
        P(None, ("wide", "patch")),
        P(),
        P(),
        P(),
        P(),
        P(),
        P(),
        P(),
        P(("wide", "patch")),
        P(("wide", "patch")),
        P(("wide", "patch"), None),
    )
    out_specs = (P(None, ("wide", "patch")), P(None, ("wide", "patch")), P())
    return jax.shard_map(body, mesh=mesh, in_specs=in_specs, out_specs=out_specs, check_vma=False)
```

```python
import functools
import math

import jax
import jax.numpy as jnp
from jax import lax
from jax.experimental import pallas as pl
from jax.experimental.pallas import tpu as pltpu
from jax.sharding import PartitionSpec as P

HEADS = 4
HEAD = 128
TILE = 128
ROWS = 88
F32 = jnp.float32
BF16 = jnp.bfloat16
MIB = 1024 * 1024
ATTEND_LIMIT = 38
SHARE = 11


def dot(a, b):
    return jnp.dot(a, b, preferred_element_type=F32)


def dot_nt(a, b):
    return lax.dot_general(a, b, (((1,), (1,)), ((), ())), preferred_element_type=F32)


def split(x):
    high = x.astype(BF16)
    return high, (x - high.astype(F32)).astype(BF16)


def call(kernel, outs, scratch, name, flops, *args, smem=(), limit=12):
    specs = [
        pl.BlockSpec(memory_space=pltpu.SMEM if i in smem else pltpu.VMEM) for i in range(len(args))
    ]
    return pl.pallas_call(
        kernel,
        out_shape=[jax.ShapeDtypeStruct(s, d) for s, d in outs],
        in_specs=specs,
        out_specs=[pl.BlockSpec(memory_space=pltpu.VMEM) for _ in outs],
        scratch_shapes=scratch,
        compiler_params=pltpu.CompilerParams(vmem_limit_bytes=limit * MIB),
        cost_estimate=pl.CostEstimate(flops=flops, bytes_accessed=1 << 20, transcendentals=0),
        name=name,
    )(*args)


def slot_targets(route):
    level = lax.broadcasted_iota(jnp.int32, (TILE, route.shape[1]), 0).astype(F32).astype(BF16)
    rank, target = route[0:1, :].astype(BF16), route[1:2, :].astype(BF16)
    return jnp.where(level == rank, target, jnp.full((), -1.0, BF16))


def slot_onehot(targets, pair, axis):
    parts = []
    for k in range(2):
        peer = (jnp.zeros((1, targets.shape[1]), F32) + (2 * pair + k).astype(F32)).astype(BF16)
        parts.append(jnp.where(targets[...] == peer, jnp.ones((), BF16), jnp.zeros((), BF16)))
    return jnp.concatenate(parts, axis=axis)


def loop(count, unroll, step):
    def some(i, _):
        for k in range(unroll):
            step(i * unroll + k)
        return 0

    lax.fori_loop(0, count // unroll, some, 0)


def pack_kernel(shift, mask, x_ref, index, out_ref, route, wide_s, pay, targets):
    variables, grid_count = x_ref.shape
    peers = out_ref.shape[0]
    chunk = 256
    upper = jnp.where(
        lax.broadcasted_iota(jnp.int32, (chunk, chunk), 0)
        < lax.broadcasted_iota(jnp.int32, (chunk, chunk), 1),
        1.0,
        0.0,
    ).astype(BF16)
    carry = jnp.zeros((peers, 1), F32)
    for start in range(0, grid_count, chunk):
        span = pl.ds(start, chunk)
        nodes = index[:, span]
        hit = lax.broadcasted_iota(jnp.int32, (peers, chunk), 0) == (nodes >> shift)
        ones = jnp.where(hit, 1.0, 0.0)
        before = dot(ones.astype(BF16), upper) + carry
        route[0:1, span] = jnp.sum(jnp.where(hit, before, 0.0), axis=0, keepdims=True)
        route[1:2, span] = (nodes >> shift).astype(F32)
        carry = carry + jnp.sum(ones, axis=1, keepdims=True)
    local = index[...] & mask
    wide_s[0:variables, :] = x_ref[...].astype(F32)
    wide_s[variables : variables + 1, :] = (local >> 1).astype(F32)
    wide_s[variables + 1 : variables + 2, :] = (local & 1).astype(F32)
    wide_s[variables + 2 : ROWS, :] = jnp.zeros((ROWS - variables - 2, grid_count), F32)
    pay[...] = wide_s[...].astype(BF16)
    targets[...] = slot_targets(route).T

    def step(pair):
        got = dot(pay[...], slot_onehot(targets, pair, 1)).astype(BF16)
        out_ref[2 * pair] = got[:, :TILE]
        out_ref[2 * pair + 1] = got[:, TILE:]

    loop(peers // 2, 4, step)


def sums_kernel(variables, recv_ref, high_ref, low_ref, index, total_ref):
    peers = recv_ref.shape[0]
    node_count = total_ref.shape[1]
    nodes = lax.broadcasted_iota(jnp.int32, (node_count, TILE), 0)
    total_ref[...] = jnp.zeros_like(total_ref)

    def step(pair):
        data, picks = [], []
        for one in range(2):
            block = recv_ref[2 * pair + one]
            wide = block[80:ROWS].astype(F32)
            at = variables - 80
            slots = (2.0 * wide[at : at + 1] + wide[at + 1 : at + 2]).astype(jnp.int32)
            index[pl.ds(2 * pair + one, 1), :] = slots
            picks.append(jnp.where(nodes == slots, 1.0, 0.0).astype(BF16))
            data.append(block)
        total_ref[...] += dot_nt(jnp.concatenate(data, axis=1), jnp.concatenate(picks, axis=1))

    loop(peers // 2, 4, step)
    keep = lax.broadcasted_iota(jnp.int32, total_ref.shape, 0) < variables
    high_ref[...], low_ref[...] = split(jnp.where(keep, total_ref[...], 0.0))


def padded(ref, rows_s):
    rows_s[...] = jnp.zeros_like(rows_s)
    rows_s[0 : ref.shape[0], :] = ref[...].astype(F32)
    return rows_s[0:ROWS, :].astype(BF16), rows_s[...].T[:, :ROWS].astype(BF16)


def column(ref):
    return jnp.broadcast_to(ref[...].astype(F32), (TILE, ref.shape[1])).T[:, :1]


def norm_t(start, gain):
    inverse = lax.rsqrt(jnp.mean(start * start, axis=0, keepdims=True) + 1e-05)
    return inverse, (start * inverse * gain).astype(BF16)


def query_kernel(high, low, enc, gain_ref, query_w, start_ref, inverse_ref, q_ref, qt_ref, rows_s):
    _, encoder_t = padded(enc, rows_s)
    start = dot(encoder_t, high[...]) + dot(encoder_t, low[...])
    start_ref[...] = start
    inverse, normed = norm_t(start, column(gain_ref))
    inverse_ref[...] = inverse
    queries = dot(query_w[...].T, normed).astype(BF16)
    qt_ref[...] = queries
    q_ref[...] = queries.T


def top_kernel(high, low, dec, output, top_ref, g_ref, gt_ref, rows_s):
    _, decoder = padded(dec, rows_s)
    top = dot(decoder, high[...]) + dot(decoder, low[...])
    top_ref[...] = top
    grad = dot(output[...], top.astype(BF16)).astype(BF16)
    gt_ref[...] = grad
    g_ref[...] = grad.T


def attend_kernel(
    place,
    pattern,
    s0_ref,
    s1_ref,
    s2_ref,
    s3_ref,
    start_ref,
    inverse_ref,
    top_ref,
    q_ref,
    qt_ref,
    g_ref,
    gt_ref,
    enc,
    gain_ref,
    query_w,
    key_w,
    value_w,
    output_w,
    dec,
    decoded_ref,
    own_ref,
    o1_ref,
    o2_ref,
    o3_ref,
    enc_ref,
    start_s,
    inverse_s,
    keys_s,
    values_s,
    weight0_s,
    weight1_s,
    prob0_s,
    prob1_s,
    score0_s,
    score1_s,
    mixed_s,
    query_s,
    keyg_s,
    valueg_s,
    rows_s,
):
    node_count = s0_ref.shape[1]
    pieces = (s0_ref, s1_ref, s2_ref, s3_ref)
    key_tiles = len(pieces) * node_count // TILE
    gain = column(gain_ref)
    _, encoder_t = padded(enc, rows_s)
    key_t = key_w[...].T
    value_t = value_w[...].T
    scale = 1.0 / math.sqrt(HEAD)
    for r, piece in enumerate(pieces):
        span = pl.ds(r * node_count, node_count)
        start = dot(encoder_t, piece[...])
        start_s[:, span] = start
        inverse, normed = norm_t(start, gain)
        inverse_s[:, span] = inverse
        keys_s[:, span] = dot(key_t, normed).astype(BF16)
        values_s[:, span] = dot(value_t, normed).astype(BF16)
    first = place[0] * (node_count // TILE)

    weight_s = (weight0_s, weight1_s)
    prob_s = (prob0_s, prob1_s)
    score_s = (score0_s, score1_s)

    def soft(h):
        rows = pl.ds(h * HEAD, HEAD)
        weight, prob = weight_s[h % 2], prob_s[h % 2]
        scores = dot(q_ref[:, rows], keys_s[rows, :])
        for qt in range(node_count // TILE):
            for kb in range(key_tiles):
                seen = pattern[qt, lax.rem(first + kb, key_tiles)] > 0
                bias = jnp.where(seen, 0.0, -1e30).astype(F32)
                at = (slice(qt * TILE, (qt + 1) * TILE), slice(kb * TILE, (kb + 1) * TILE))
                weight[at] = scores[at] * (scale / math.log(2.0)) + bias
        biased = weight[...]
        weights = jnp.exp2(biased - jnp.max(biased, axis=1, keepdims=True))
        probs = weights * (1.0 / jnp.sum(weights, axis=1, keepdims=True))
        weight[...] = probs
        prob[...] = probs.astype(BF16)

    def rest(h):
        rows = pl.ds(h * HEAD, HEAD)
        weight, prob, score = weight_s[h % 2], prob_s[h % 2], score_s[h % 2]
        g, kt, vt = g_ref[:, rows], keys_s[rows, :], values_s[rows, :]
        mixed = dot_nt(prob[...], vt)
        mixed_s[rows, :] = mixed.astype(BF16).T
        delta = jnp.sum(mixed * g.astype(F32), axis=1, keepdims=True)
        prob_grad = dot(g, vt)
        score[...] = (weight[...] * ((prob_grad - delta) * scale)).astype(BF16)
        query_s[rows, :] = dot_nt(score[...], kt).astype(BF16).T
        keyg_s[rows, :] = dot(qt_ref[rows, :], score[...]).astype(BF16)
        valueg_s[rows, :] = dot(gt_ref[rows, :], prob[...]).astype(BF16)

    soft(0)
    for h in range(HEADS):
        if h + 1 < HEADS:
            soft(h + 1)
        rest(h)
    final = start_ref[...] + dot(output_w[...].T, mixed_s[...])
    decoder_t, _ = padded(dec, rows_s)
    decoded_ref[...] = dot(decoder_t, final.astype(BF16)).astype(BF16)
    encoder, _ = padded(enc, rows_s)
    total_enc = jnp.zeros(enc_ref.shape, F32)
    for r, (piece, out) in enumerate(zip(pieces, (own_ref, o1_ref, o2_ref, o3_ref))):
        span = pl.ds(r * node_count, node_count)
        grad = dot(key_w[...], keyg_s[:, span]) + dot(value_w[...], valueg_s[:, span])
        if r == 0:
            grad = grad + dot(query_w[...], query_s[...])
            start, inverse = start_ref[...], inverse_ref[...]
        else:
            start, inverse = start_s[:, span], inverse_s[:, span]
        scaled = grad * gain
        mean = jnp.mean(start * scaled, axis=0, keepdims=True)
        total = inverse * scaled - start * (inverse * inverse * inverse * mean)
        if r == 0:
            total = total + top_ref[...]
        total = total.astype(BF16)
        out[...] = dot(encoder, total).astype(out.dtype)
        total_enc = total_enc + dot_nt(piece[...], total)
    enc_ref[...] = total_enc


def picks_of(index, pair, nodes):
    return jnp.concatenate(
        [
            jnp.where(nodes == index[pl.ds(2 * pair + one, 1), :], 1.0, 0.0).astype(BF16)
            for one in range(2)
        ],
        axis=1,
    )


def decoded_slots_kernel(index, decoded_ref, enc_ref, out_ref, whole, extra):
    peers = out_ref.shape[0]
    height = enc_ref.shape[0]
    for t in range(enc_ref.shape[1] // TILE):
        whole[t * height : (t + 1) * height, :] = enc_ref[:, t * TILE : (t + 1) * TILE]
    extra[...] = jnp.zeros_like(extra)
    for j in range(SHARE):
        extra[pl.ds(4 + j, peers, stride=16), :] = whole[j * peers : (j + 1) * peers, :]
    nodes = lax.broadcasted_iota(jnp.int32, (decoded_ref.shape[1], TILE), 0)

    def step(pair):
        got = dot(decoded_ref[...], picks_of(index, pair, nodes))
        for one in range(2):
            tail = extra[pl.ds(pl.multiple_of((2 * pair + one) * 16, 16), 16), :]
            rows = got[:, one * TILE : (one + 1) * TILE]
            rows = jnp.concatenate([rows[:80], rows[80:] + tail[:8], tail[8:]], axis=0)
            out_ref[2 * pair + one] = rows.astype(BF16)

    loop(peers // 2, 4, step)


def grad_slots_kernel(index, own_ref, i1_ref, i2_ref, i3_ref, out_ref, grad_s):
    total = own_ref[...]
    for piece in (i1_ref, i2_ref, i3_ref):
        total = total + piece[...].astype(F32)
    grad_s[...] = total.astype(BF16)
    nodes = lax.broadcasted_iota(jnp.int32, (own_ref.shape[1], TILE), 0)
    blank = jnp.zeros((out_ref.shape[1] - ROWS, TILE), F32)

    def step(pair):
        got = dot(grad_s[...], picks_of(index, pair, nodes))
        for one in range(2):
            rows = jnp.concatenate([got[:, one * TILE : (one + 1) * TILE], blank], axis=0)
            out_ref[2 * pair + one] = rows.astype(BF16)

    loop(out_ref.shape[0] // 2, 4, step)


def unpack_kernel(back_ref, route, out_ref, acc, targets):
    peers = back_ref.shape[0]
    targets[...] = slot_targets(route)
    acc[...] = jnp.zeros_like(acc)

    def step(pair):
        data = jnp.concatenate([back_ref[2 * pair], back_ref[2 * pair + 1]], axis=1)
        acc[...] += dot(data[:ROWS], slot_onehot(targets, pair, 0))

    loop(peers // 2, 4, step)
    out_ref[...] = acc[0 : out_ref.shape[0], :].astype(out_ref.dtype)


def assemble_kernel(p0_ref, p1_ref, p2_ref, p3_ref, out_ref):
    total = p0_ref[...].astype(F32)
    for part in (p1_ref, p2_ref, p3_ref):
        total = total + part[...].astype(F32)
    for t in range(out_ref.shape[1] // TILE):
        rows = total[t * ROWS : (t + 1) * ROWS]
        out_ref[:, t * TILE : (t + 1) * TILE] = rows[: out_ref.shape[0]]


def body(
    grid_state,
    cotangent,
    encoder_weight,
    norm_gain,
    query_weight,
    key_weight,
    value_weight,
    output_weight,
    decoder_weight,
    grid_owner,
    decode_node,
    tile_pattern,
):
    peers = lax.axis_size("wide")
    group = lax.axis_size("patch")
    variables, grid_count = grid_state.shape
    width = query_weight.shape[0]
    nodes = tile_pattern.shape[0] * TILE
    keys = group * nodes
    capacity = 2 * grid_count // peers
    shift = (nodes * group).bit_length() - 1
    vm = pltpu.VMEM

    route = 2 * ROWS * grid_count * peers * capacity
    spread = 2 * ROWS * nodes * peers * capacity

    def exchange(x):
        return lax.all_to_all(x, "wide", split_axis=0, concat_axis=0, tiled=True)

    def pack(x, index):
        return call(
            functools.partial(pack_kernel, shift, nodes - 1),
            [((peers, ROWS, capacity), BF16), ((2, grid_count), F32)],
            [
                vm((ROWS, grid_count), F32),
                vm((ROWS, grid_count), BF16),
                vm((grid_count, capacity), BF16),
            ],
            "pack",
            route,
            x,
            index.reshape(1, grid_count),
        )

    def sums(recv):
        return call(
            functools.partial(sums_kernel, variables),
            [((ROWS, nodes), BF16), ((ROWS, nodes), BF16), ((peers, capacity), jnp.int32)],
            [vm((ROWS, nodes), F32)],
            "sums",
            spread,
            recv,
        )

    def unpack(x, slots, dtype):
        return call(
            unpack_kernel,
            [((variables, grid_count), dtype)],
            [vm((ROWS, grid_count), F32), vm((capacity, grid_count), BF16)],
            "unpack",
            route,
            x,
            slots,
        )[0]

    def from_ahead(x, r):
        return lax.ppermute(x, "patch", [((i + r) % group, i) for i in range(group)])

    def to_ahead(x, r):
        return lax.ppermute(x, "patch", [(i, (i + r) % group) for i in range(group)])

    place = lax.axis_index("patch").reshape(1).astype(jnp.int32)
    gain = norm_gain.reshape(1, width)
    decoder_rows = decoder_weight.T

    state_send, own_slots = pack(grid_state, grid_owner)
    cotangent, state_send = lax.optimization_barrier((cotangent, state_send))
    state_recv = exchange(state_send)
    cot_send, dec_slots = pack(cotangent, decode_node)
    cot_recv = exchange(cot_send)

    state, state_low, own_idx = sums(state_recv)
    pieces = [state] + [from_ahead(state, r) for r in range(1, group)]
    square = ((width, nodes), BF16)
    start, inverse, q, qt = call(
        query_kernel,
        [((width, nodes), F32), ((1, nodes), F32), square, square],
        [vm((TILE, width), F32)],
        "query",
        3 * width * width * nodes,
        state,
        state_low,
        encoder_weight,
        gain,
        query_weight,
    )
    cot, cot_low, dec_idx = sums(cot_recv)
    top, g, gt = call(
        top_kernel,
        [((width, nodes), F32), square, square],
        [vm((TILE, width), F32)],
        "top",
        3 * width * width * nodes,
        cot,
        cot_low,
        decoder_rows,
        output_weight,
    )
    decoded, own, o1, o2, o3, enc = call(
        attend_kernel,
        [((ROWS, nodes), BF16), ((ROWS, nodes), F32)]
        + [((ROWS, nodes), BF16)] * 3
        + [((ROWS, width), F32)],
        [
            vm((width, keys), F32),
            vm((1, keys), F32),
            vm((width, keys), BF16),
            vm((width, keys), BF16),
            vm((nodes, keys), F32),
            vm((nodes, keys), F32),
            vm((nodes, keys), BF16),
            vm((nodes, keys), BF16),
            vm((nodes, keys), BF16),
            vm((nodes, keys), BF16),
            vm((width, nodes), BF16),
            vm((width, nodes), BF16),
            vm((width, keys), BF16),
            vm((width, keys), BF16),
            vm((TILE, width), F32),
        ],
        "attend",
        20 * nodes * keys * width,
        place,
        tile_pattern,
        *pieces,
        start,
        inverse,
        top,
        q,
        qt,
        g,
        gt,
        encoder_weight,
        gain,
        query_weight,
        key_weight,
        value_weight,
        output_weight,
        decoder_rows,
        smem=(0, 1),
        limit=ATTEND_LIMIT,
    )
    back = [to_ahead(o, r) for r, o in ((1, o1), (2, o2), (3, o3))]
    (decoded_send,) = call(
        decoded_slots_kernel,
        [((peers, ROWS + 8, capacity), BF16)],
        [vm((peers * SHARE, TILE), F32), vm((peers * 16, TILE), F32)],
        "decoded_slots",
        spread,
        dec_idx,
        decoded,
        enc,
    )
    decoded_back = exchange(decoded_send)
    (grad_send,) = call(
        grad_slots_kernel,
        [((peers, ROWS + 8, capacity), BF16)],
        [vm((ROWS, nodes), BF16)],
        "grad_slots",
        spread,
        own_idx,
        own,
        *back,
    )
    span = slice(variables, variables + SHARE)
    chunk = jnp.sum(decoded_back[:, span].astype(F32), axis=0).astype(BF16)
    chunk = jnp.broadcast_to(chunk, (peers,) + chunk.shape)
    grad_send = lax.dynamic_update_slice(grad_send, chunk, (0, variables, 0))
    grad_back = exchange(grad_send)
    denoised = unpack(decoded_back, dec_slots, BF16)
    grad_back, denoised = lax.optimization_barrier((grad_back, denoised))
    mine = jnp.swapaxes(grad_back[:, span], 0, 1).reshape(peers * SHARE, TILE)
    parts = [mine] + [from_ahead(mine, r) for r in range(1, group)]
    state_grad = unpack(grad_back, own_slots, F32)
    (encoder_grad,) = call(
        assemble_kernel, [((variables, width), F32)], [], "assemble", 8 * ROWS * width, *parts
    )
    return (denoised, state_grad, encoder_grad)


def solution(mesh):
    in_specs = (
        P(None, ("wide", "patch")),
        P(None, ("wide", "patch")),
        P(),
        P(),
        P(),
        P(),
        P(),
        P(),
        P(),
        P(("wide", "patch")),
        P(("wide", "patch")),
        P(("wide", "patch"), None),
    )
    out_specs = (P(None, ("wide", "patch")), P(None, ("wide", "patch")), P())
    return jax.shard_map(body, mesh=mesh, in_specs=in_specs, out_specs=out_specs, check_vma=False)
```

```python
import functools
import math

import jax
import jax.numpy as jnp
from jax import lax
from jax.experimental import pallas as pl
from jax.experimental.pallas import tpu as pltpu
from jax.sharding import PartitionSpec as P

HEADS = 4
HEAD = 128
TILE = 128
ROWS = 88
F32 = jnp.float32
BF16 = jnp.bfloat16
MIB = 1024 * 1024
ATTEND_LIMIT = 38
SHARE = 11


def dot(a, b):
    return jnp.dot(a, b, preferred_element_type=F32)


def dot_nt(a, b):
    return lax.dot_general(a, b, (((1,), (1,)), ((), ())), preferred_element_type=F32)


def split(x):
    high = x.astype(BF16)
    return high, (x - high.astype(F32)).astype(BF16)


def call(kernel, outs, scratch, name, flops, *args, smem=(), limit=12):
    specs = [
        pl.BlockSpec(memory_space=pltpu.SMEM if i in smem else pltpu.VMEM) for i in range(len(args))
    ]
    return pl.pallas_call(
        kernel,
        out_shape=[jax.ShapeDtypeStruct(s, d) for s, d in outs],
        in_specs=specs,
        out_specs=[pl.BlockSpec(memory_space=pltpu.VMEM) for _ in outs],
        scratch_shapes=scratch,
        compiler_params=pltpu.CompilerParams(vmem_limit_bytes=limit * MIB),
        cost_estimate=pl.CostEstimate(flops=flops, bytes_accessed=1 << 20, transcendentals=0),
        name=name,
    )(*args)


def slot_targets(route):
    level = lax.broadcasted_iota(jnp.int32, (TILE, route.shape[1]), 0).astype(F32).astype(BF16)
    rank, target = route[0:1, :].astype(BF16), route[1:2, :].astype(BF16)
    return jnp.where(level == rank, target, jnp.full((), -1.0, BF16))


def slot_onehot(targets, pair, axis):
    parts = []
    for k in range(2):
        peer = (jnp.zeros((1, targets.shape[1]), F32) + (2 * pair + k).astype(F32)).astype(BF16)
        parts.append(jnp.where(targets[...] == peer, jnp.ones((), BF16), jnp.zeros((), BF16)))
    return jnp.concatenate(parts, axis=axis)


def loop(count, unroll, step):
    def some(i, _):
        for k in range(unroll):
            step(i * unroll + k)
        return 0

    lax.fori_loop(0, count // unroll, some, 0)


def pack_kernel(shift, mask, x_ref, index, out_ref, route, wide_s, pay, targets):
    variables, grid_count = x_ref.shape
    peers = out_ref.shape[0]
    chunk = 256
    upper = jnp.where(
        lax.broadcasted_iota(jnp.int32, (chunk, chunk), 0)
        < lax.broadcasted_iota(jnp.int32, (chunk, chunk), 1),
        1.0,
        0.0,
    ).astype(BF16)
    carry = jnp.zeros((peers, 1), F32)
    for start in range(0, grid_count, chunk):
        span = pl.ds(start, chunk)
        nodes = index[:, span]
        hit = lax.broadcasted_iota(jnp.int32, (peers, chunk), 0) == (nodes >> shift)
        ones = jnp.where(hit, 1.0, 0.0)
        before = dot(ones.astype(BF16), upper) + carry
        route[0:1, span] = jnp.sum(jnp.where(hit, before, 0.0), axis=0, keepdims=True)
        route[1:2, span] = (nodes >> shift).astype(F32)
        carry = carry + jnp.sum(ones, axis=1, keepdims=True)
    local = index[...] & mask
    wide_s[0:variables, :] = x_ref[...].astype(F32)
    wide_s[variables : variables + 1, :] = (local >> 1).astype(F32)
    wide_s[variables + 1 : variables + 2, :] = (local & 1).astype(F32)
    wide_s[variables + 2 : ROWS, :] = jnp.zeros((ROWS - variables - 2, grid_count), F32)
    pay[...] = wide_s[...].astype(BF16)
    targets[...] = slot_targets(route).T

    def step(pair):
        got = dot(pay[...], slot_onehot(targets, pair, 1)).astype(BF16)
        out_ref[2 * pair] = got[:, :TILE]
        out_ref[2 * pair + 1] = got[:, TILE:]

    loop(peers // 2, 8, step)


def sums_kernel(variables, recv_ref, high_ref, low_ref, index, total_ref):
    peers = recv_ref.shape[0]
    node_count = total_ref.shape[1]
    nodes = lax.broadcasted_iota(jnp.int32, (node_count, TILE), 0)
    total_ref[...] = jnp.zeros_like(total_ref)

    def step(pair):
        data, picks = [], []
        for one in range(2):
            block = recv_ref[2 * pair + one]
            wide = block[80:ROWS].astype(F32)
            at = variables - 80
            slots = (2.0 * wide[at : at + 1] + wide[at + 1 : at + 2]).astype(jnp.int32)
            index[pl.ds(2 * pair + one, 1), :] = slots
            picks.append(jnp.where(nodes == slots, 1.0, 0.0).astype(BF16))
            data.append(block)
        total_ref[...] += dot_nt(jnp.concatenate(data, axis=1), jnp.concatenate(picks, axis=1))

    loop(peers // 2, 8, step)
    keep = lax.broadcasted_iota(jnp.int32, total_ref.shape, 0) < variables
    high_ref[...], low_ref[...] = split(jnp.where(keep, total_ref[...], 0.0))


def padded(ref, rows_s):
    rows_s[...] = jnp.zeros_like(rows_s)
    rows_s[0 : ref.shape[0], :] = ref[...].astype(F32)
    return rows_s[0:ROWS, :].astype(BF16), rows_s[...].T[:, :ROWS].astype(BF16)


def column(ref):
    return jnp.broadcast_to(ref[...].astype(F32), (TILE, ref.shape[1])).T[:, :1]


def norm_t(start, gain):
    inverse = lax.rsqrt(jnp.mean(start * start, axis=0, keepdims=True) + 1e-05)
    return inverse, (start * inverse * gain).astype(BF16)


def query_kernel(high, low, enc, gain_ref, query_w, start_ref, inverse_ref, q_ref, qt_ref, rows_s):
    _, encoder_t = padded(enc, rows_s)
    start = dot(encoder_t, high[...]) + dot(encoder_t, low[...])
    start_ref[...] = start
    inverse, normed = norm_t(start, column(gain_ref))
    inverse_ref[...] = inverse
    queries = dot(query_w[...].T, normed).astype(BF16)
    qt_ref[...] = queries
    q_ref[...] = queries.T


def top_kernel(high, low, dec, output, top_ref, g_ref, gt_ref, rows_s):
    _, decoder = padded(dec, rows_s)
    top = dot(decoder, high[...]) + dot(decoder, low[...])
    top_ref[...] = top
    grad = dot(output[...], top.astype(BF16)).astype(BF16)
    gt_ref[...] = grad
    g_ref[...] = grad.T


def attend_kernel(
    place,
    pattern,
    s0_ref,
    s1_ref,
    s2_ref,
    s3_ref,
    start_ref,
    inverse_ref,
    top_ref,
    q_ref,
    qt_ref,
    g_ref,
    gt_ref,
    enc,
    gain_ref,
    query_w,
    key_w,
    value_w,
    output_w,
    dec,
    decoded_ref,
    own_ref,
    o1_ref,
    o2_ref,
    o3_ref,
    enc_ref,
    start_s,
    inverse_s,
    keys_s,
    values_s,
    weight0_s,
    weight1_s,
    prob0_s,
    prob1_s,
    score0_s,
    score1_s,
    mixed_s,
    query_s,
    keyg_s,
    valueg_s,
    rows_s,
):
    node_count = s0_ref.shape[1]
    pieces = (s0_ref, s1_ref, s2_ref, s3_ref)
    key_tiles = len(pieces) * node_count // TILE
    gain = column(gain_ref)
    _, encoder_t = padded(enc, rows_s)
    key_t = key_w[...].T
    value_t = value_w[...].T
    scale = 1.0 / math.sqrt(HEAD)
    for r, piece in enumerate(pieces):
        span = pl.ds(r * node_count, node_count)
        start = dot(encoder_t, piece[...])
        start_s[:, span] = start
        inverse, normed = norm_t(start, gain)
        inverse_s[:, span] = inverse
        keys_s[:, span] = dot(key_t, normed).astype(BF16)
        values_s[:, span] = dot(value_t, normed).astype(BF16)
    first = place[0] * (node_count // TILE)

    weight_s = (weight0_s, weight1_s)
    prob_s = (prob0_s, prob1_s)
    score_s = (score0_s, score1_s)

    def soft(h):
        rows = pl.ds(h * HEAD, HEAD)
        weight, prob = weight_s[h % 2], prob_s[h % 2]
        scores = dot(q_ref[:, rows], keys_s[rows, :])
        for qt in range(node_count // TILE):
            for kb in range(key_tiles):
                seen = pattern[qt, lax.rem(first + kb, key_tiles)] > 0
                bias = jnp.where(seen, 0.0, -1e30).astype(F32)
                at = (slice(qt * TILE, (qt + 1) * TILE), slice(kb * TILE, (kb + 1) * TILE))
                weight[at] = scores[at] * (scale / math.log(2.0)) + bias
        biased = weight[...]
        weights = jnp.exp2(biased - jnp.max(biased, axis=1, keepdims=True))
        probs = weights * (1.0 / jnp.sum(weights, axis=1, keepdims=True))
        weight[...] = probs
        prob[...] = probs.astype(BF16)

    def rest(h):
        rows = pl.ds(h * HEAD, HEAD)
        weight, prob, score = weight_s[h % 2], prob_s[h % 2], score_s[h % 2]
        g, kt, vt = g_ref[:, rows], keys_s[rows, :], values_s[rows, :]
        mixed = dot_nt(prob[...], vt)
        mixed_s[rows, :] = mixed.astype(BF16).T
        delta = jnp.sum(mixed * g.astype(F32), axis=1, keepdims=True)
        prob_grad = dot(g, vt)
        score[...] = (weight[...] * ((prob_grad - delta) * scale)).astype(BF16)
        query_s[rows, :] = dot_nt(score[...], kt).astype(BF16).T
        keyg_s[rows, :] = dot(qt_ref[rows, :], score[...]).astype(BF16)
        valueg_s[rows, :] = dot(gt_ref[rows, :], prob[...]).astype(BF16)

    soft(0)
    for h in range(HEADS):
        if h + 1 < HEADS:
            soft(h + 1)
        rest(h)
    final = start_ref[...] + dot(output_w[...].T, mixed_s[...])
    decoder_t, _ = padded(dec, rows_s)
    decoded_ref[...] = dot(decoder_t, final.astype(BF16)).astype(BF16)
    encoder, _ = padded(enc, rows_s)
    total_enc = jnp.zeros(enc_ref.shape, F32)
    for r, (piece, out) in enumerate(zip(pieces, (own_ref, o1_ref, o2_ref, o3_ref))):
        span = pl.ds(r * node_count, node_count)
        grad = dot(key_w[...], keyg_s[:, span]) + dot(value_w[...], valueg_s[:, span])
        if r == 0:
            grad = grad + dot(query_w[...], query_s[...])
            start, inverse = start_ref[...], inverse_ref[...]
        else:
            start, inverse = start_s[:, span], inverse_s[:, span]
        scaled = grad * gain
        mean = jnp.mean(start * scaled, axis=0, keepdims=True)
        total = inverse * scaled - start * (inverse * inverse * inverse * mean)
        if r == 0:
            total = total + top_ref[...]
        total = total.astype(BF16)
        out[...] = dot(encoder, total).astype(out.dtype)
        total_enc = total_enc + dot_nt(piece[...], total)
    enc_ref[...] = total_enc


def picks_of(index, pair, nodes):
    return jnp.concatenate(
        [
            jnp.where(nodes == index[pl.ds(2 * pair + one, 1), :], 1.0, 0.0).astype(BF16)
            for one in range(2)
        ],
        axis=1,
    )


def decoded_slots_kernel(index, decoded_ref, enc_ref, out_ref, whole, extra):
    peers = out_ref.shape[0]
    height = enc_ref.shape[0]
    for t in range(enc_ref.shape[1] // TILE):
        whole[t * height : (t + 1) * height, :] = enc_ref[:, t * TILE : (t + 1) * TILE]
    extra[...] = jnp.zeros_like(extra)
    for j in range(SHARE):
        extra[pl.ds(4 + j, peers, stride=16), :] = whole[j * peers : (j + 1) * peers, :]
    nodes = lax.broadcasted_iota(jnp.int32, (decoded_ref.shape[1], TILE), 0)

    def step(pair):
        got = dot(decoded_ref[...], picks_of(index, pair, nodes))
        for one in range(2):
            tail = extra[pl.ds(pl.multiple_of((2 * pair + one) * 16, 16), 16), :]
            rows = got[:, one * TILE : (one + 1) * TILE]
            rows = jnp.concatenate([rows[:80], rows[80:] + tail[:8], tail[8:]], axis=0)
            out_ref[2 * pair + one] = rows.astype(BF16)

    loop(peers // 2, 8, step)


def grad_slots_kernel(index, own_ref, i1_ref, i2_ref, i3_ref, out_ref, grad_s):
    total = own_ref[...]
    for piece in (i1_ref, i2_ref, i3_ref):
        total = total + piece[...].astype(F32)
    grad_s[...] = total.astype(BF16)
    nodes = lax.broadcasted_iota(jnp.int32, (own_ref.shape[1], TILE), 0)
    blank = jnp.zeros((out_ref.shape[1] - ROWS, TILE), F32)

    def step(pair):
        got = dot(grad_s[...], picks_of(index, pair, nodes))
        for one in range(2):
            rows = jnp.concatenate([got[:, one * TILE : (one + 1) * TILE], blank], axis=0)
            out_ref[2 * pair + one] = rows.astype(BF16)

    loop(out_ref.shape[0] // 2, 8, step)


def unpack_kernel(back_ref, route, out_ref, acc, targets):
    peers = back_ref.shape[0]
    targets[...] = slot_targets(route)
    acc[...] = jnp.zeros_like(acc)

    def step(pair):
        data = jnp.concatenate([back_ref[2 * pair], back_ref[2 * pair + 1]], axis=1)
        acc[...] += dot(data[:ROWS], slot_onehot(targets, pair, 0))

    loop(peers // 2, 8, step)
    out_ref[...] = acc[0 : out_ref.shape[0], :].astype(out_ref.dtype)


def assemble_kernel(p0_ref, p1_ref, p2_ref, p3_ref, out_ref):
    total = p0_ref[...].astype(F32)
    for part in (p1_ref, p2_ref, p3_ref):
        total = total + part[...].astype(F32)
    for t in range(out_ref.shape[1] // TILE):
        rows = total[t * ROWS : (t + 1) * ROWS]
        out_ref[:, t * TILE : (t + 1) * TILE] = rows[: out_ref.shape[0]]


def body(
    grid_state,
    cotangent,
    encoder_weight,
    norm_gain,
    query_weight,
    key_weight,
    value_weight,
    output_weight,
    decoder_weight,
    grid_owner,
    decode_node,
    tile_pattern,
):
    peers = lax.axis_size("wide")
    group = lax.axis_size("patch")
    variables, grid_count = grid_state.shape
    width = query_weight.shape[0]
    nodes = tile_pattern.shape[0] * TILE
    keys = group * nodes
    capacity = 2 * grid_count // peers
    shift = (nodes * group).bit_length() - 1
    vm = pltpu.VMEM

    route = 2 * ROWS * grid_count * peers * capacity
    spread = 2 * ROWS * nodes * peers * capacity

    def exchange(x):
        return lax.all_to_all(x, "wide", split_axis=0, concat_axis=0, tiled=True)

    def pack(x, index):
        return call(
            functools.partial(pack_kernel, shift, nodes - 1),
            [((peers, ROWS, capacity), BF16), ((2, grid_count), F32)],
            [
                vm((ROWS, grid_count), F32),
                vm((ROWS, grid_count), BF16),
                vm((grid_count, capacity), BF16),
            ],
            "pack",
            route,
            x,
            index.reshape(1, grid_count),
        )

    def sums(recv):
        return call(
            functools.partial(sums_kernel, variables),
            [((ROWS, nodes), BF16), ((ROWS, nodes), BF16), ((peers, capacity), jnp.int32)],
            [vm((ROWS, nodes), F32)],
            "sums",
            spread,
            recv,
        )

    def unpack(x, slots, dtype):
        return call(
            unpack_kernel,
            [((variables, grid_count), dtype)],
            [vm((ROWS, grid_count), F32), vm((capacity, grid_count), BF16)],
            "unpack",
            route,
            x,
            slots,
        )[0]

    def from_ahead(x, r):
        return lax.ppermute(x, "patch", [((i + r) % group, i) for i in range(group)])

    def to_ahead(x, r):
        return lax.ppermute(x, "patch", [(i, (i + r) % group) for i in range(group)])

    place = lax.axis_index("patch").reshape(1).astype(jnp.int32)
    gain = norm_gain.reshape(1, width)
    decoder_rows = decoder_weight.T

    state_send, own_slots = pack(grid_state, grid_owner)
    cotangent, state_send = lax.optimization_barrier((cotangent, state_send))
    state_recv = exchange(state_send)
    cot_send, dec_slots = pack(cotangent, decode_node)
    cot_recv = exchange(cot_send)

    state, state_low, own_idx = sums(state_recv)
    pieces = [state] + [from_ahead(state, r) for r in range(1, group)]
    square = ((width, nodes), BF16)
    start, inverse, q, qt = call(
        query_kernel,
        [((width, nodes), F32), ((1, nodes), F32), square, square],
        [vm((TILE, width), F32)],
        "query",
        3 * width * width * nodes,
        state,
        state_low,
        encoder_weight,
        gain,
        query_weight,
    )
    cot, cot_low, dec_idx = sums(cot_recv)
    top, g, gt = call(
        top_kernel,
        [((width, nodes), F32), square, square],
        [vm((TILE, width), F32)],
        "top",
        3 * width * width * nodes,
        cot,
        cot_low,
        decoder_rows,
        output_weight,
    )
    decoded, own, o1, o2, o3, enc = call(
        attend_kernel,
        [((ROWS, nodes), BF16), ((ROWS, nodes), F32)]
        + [((ROWS, nodes), BF16)] * 3
        + [((ROWS, width), F32)],
        [
            vm((width, keys), F32),
            vm((1, keys), F32),
            vm((width, keys), BF16),
            vm((width, keys), BF16),
            vm((nodes, keys), F32),
            vm((nodes, keys), F32),
            vm((nodes, keys), BF16),
            vm((nodes, keys), BF16),
            vm((nodes, keys), BF16),
            vm((nodes, keys), BF16),
            vm((width, nodes), BF16),
            vm((width, nodes), BF16),
            vm((width, keys), BF16),
            vm((width, keys), BF16),
            vm((TILE, width), F32),
        ],
        "attend",
        20 * nodes * keys * width,
        place,
        tile_pattern,
        *pieces,
        start,
        inverse,
        top,
        q,
        qt,
        g,
        gt,
        encoder_weight,
        gain,
        query_weight,
        key_weight,
        value_weight,
        output_weight,
        decoder_rows,
        smem=(0, 1),
        limit=ATTEND_LIMIT,
    )
    back = [to_ahead(o, r) for r, o in ((1, o1), (2, o2), (3, o3))]
    (decoded_send,) = call(
        decoded_slots_kernel,
        [((peers, ROWS + 8, capacity), BF16)],
        [vm((peers * SHARE, TILE), F32), vm((peers * 16, TILE), F32)],
        "decoded_slots",
        spread,
        dec_idx,
        decoded,
        enc,
    )
    decoded_back = exchange(decoded_send)
    (grad_send,) = call(
        grad_slots_kernel,
        [((peers, ROWS + 8, capacity), BF16)],
        [vm((ROWS, nodes), BF16)],
        "grad_slots",
        spread,
        own_idx,
        own,
        *back,
    )
    span = slice(variables, variables + SHARE)
    chunk = jnp.sum(decoded_back[:, span].astype(F32), axis=0).astype(BF16)
    chunk = jnp.broadcast_to(chunk, (peers,) + chunk.shape)
    grad_send = lax.dynamic_update_slice(grad_send, chunk, (0, variables, 0))
    grad_back = exchange(grad_send)
    denoised = unpack(decoded_back, dec_slots, BF16)
    grad_back, denoised = lax.optimization_barrier((grad_back, denoised))
    mine = jnp.swapaxes(grad_back[:, span], 0, 1).reshape(peers * SHARE, TILE)
    parts = [mine] + [from_ahead(mine, r) for r in range(1, group)]
    state_grad = unpack(grad_back, own_slots, F32)
    (encoder_grad,) = call(
        assemble_kernel, [((variables, width), F32)], [], "assemble", 8 * ROWS * width, *parts
    )
    return (denoised, state_grad, encoder_grad)


def solution(mesh):
    in_specs = (
        P(None, ("wide", "patch")),
        P(None, ("wide", "patch")),
        P(),
        P(),
        P(),
        P(),
        P(),
        P(),
        P(),
        P(("wide", "patch")),
        P(("wide", "patch")),
        P(("wide", "patch"), None),
    )
    out_specs = (P(None, ("wide", "patch")), P(None, ("wide", "patch")), P())
    return jax.shard_map(body, mesh=mesh, in_specs=in_specs, out_specs=out_specs, check_vma=False)
```
